512 devices in a mesh: sec: 2 (over core), blk: 128 (over x, y, z_lo), lev: 2 (over z_hi).
Axes of the slice: x: 4, y: 8, z: 8 (z_hi: 2, z_lo: 4; z = z_hi * 4 + z_lo), core: 2. Of those that a mesh axis runs over, the one named last changes fastest.
Arguments:
- state: float32 [1024, 32, 1536], P('blk', 'sec', 'lev'), may hold values from -6 to 6
- u_wind: float32 [1024, 32, 128], P('blk', 'sec', 'lev'), may hold values from -4 to 4
- v_wind: float32 [1024, 32, 128], P('blk', 'sec', 'lev'), may hold values from -4 to 4
- mixing: float32 [128, 128], replicated, may hold values from -1 to 2
- stretch_order: int32 [32768], P(('sec', 'blk')), may hold values from 0 to 127, as said below
- remap_index: int32 [65536, 4], P(('sec', 'blk', 'lev')), may hold values from 0 to 127
- remap_weight: float32 [65536, 4], P(('sec', 'blk', 'lev')), may hold values from 0.1 to 1
- land_sea: int32 [65536], P(('sec', 'blk', 'lev')), may hold values 0 or 1
- ocean_temp: float32 [80, 65536], P(None, ('sec', 'blk', 'lev')), may hold values from -6 to 6
- ocean_mixing: float32 [80, 80], replicated, may hold values from -1 to 2
Outputs:
- advanced_model_quantities: float32 [1024, 32, 1536], P('blk', 'sec', 'lev')
- parameterized_rate_per_line: float32 [32768, 128], P(('sec', 'blk', 'lev'))
- physics_row_fields: float32 [32768, 1536], P(('sec', 'blk', 'lev'))
- refreshed_sea_depth_curves: float32 [80, 65536], P(None, ('sec', 'blk', 'lev'))
- sst_atm: float32 [1024, 32], P('blk', 'sec')
The draws below stay inside these ranges and needn't reach their ends.
Inputs may be any that keep to these rules, and one draw needn't show every extreme that they name: `stretch_order`: each aligned block of 128 entries is a permutation of 0 to 127.
All inputs are finite; a program needn't handle non-finite values. No bound on the sum of `land_sea` on one device may be relied on, other than what follows from the above.
Results may differ from the reference program's by a relative error of at most 0.0001.
Values sent between devices are 32-bit elements; how exact they have to be, the bound alone decides.
A program may use at most 64 MiB of HBM per device.

```python
import math
import jax
import jax.numpy as jnp
import numpy as np
from jax import lax

NP = 4
XPTS = 8
YPTS = 16
STRIP_NODE_COUNT = 1024
TRANSVERSE_NODES = 32
LEV = 128
NF = 12
COLS = 128
STRETCH = 64
SHARE = 1
OLEV = 80
OC = 128
OCELLS = 65536
REMAP = 4
N_SEC = 2
N_BLK = 128
N_LEV = 2


def square_operator(key, order, broadcast_entries):
    noise = jax.random.uniform(key, (order, order), jnp.float32, -1.0, 1.0) * (broadcast_entries / math.sqrt(order))
    identity = jnp.eye(order, dtype=jnp.float32)
    return identity + noise * (1.0 - identity)


def draw_mixing(key, part):
    key = jax.random.fold_in(key, 2)
    return square_operator(key, LEV, 0.8)


def draw_ocean_mixing(key, part):
    key = jax.random.fold_in(key, 3)
    return square_operator(key, OLEV, 0.8)


def draw_stretch_order(key, part):
    key = jax.random.fold_in(key, 1)
    keys = jax.random.split(key, N_SEC * N_BLK)
    orders = jax.vmap(lambda single: jax.random.permutation(single, COLS))(keys)
    return orders.reshape(-1).astype(jnp.int32)


def set_ends(drawn, own_key, low, high):
    longest = drawn.shape.index(max(drawn.shape))
    spots = []
    for shift in (0, 1):
        where = [jax.random.randint(jax.random.fold_in(own_key, axis), (), 0, length) for axis, length in enumerate(drawn.shape)]
        where[longest] = (where[longest] + shift) % drawn.shape[longest]
        spots.append(tuple(where))
    return drawn.at[spots[0]].set(low).at[spots[1]].set(high)


def shard_levels(own_key, dims, cuts, low, top_value):
    def one(position, blocks):
        draws = jax.random.uniform(jax.random.fold_in(jax.random.fold_in(own_key, 6), position), (blocks,), jnp.float32, low / len(cuts), top_value / len(cuts))
        return jnp.repeat(jnp.exp(draws), dims[position] // blocks).reshape((-1,) + (1,) * (len(dims) - position - 1))

    factor_of = one(*cuts[0])
    for cut in cuts[1:]:
        factor_of = factor_of * one(*cut)
    return factor_of


def bell_draw(key, extent, width, limit, cuts=(), kind=jnp.bfloat16):
    values = jax.random.normal(key, extent, jnp.float32) * width
    if len(cuts) > 0:
        values = shard_levels(key, extent, cuts, -0.22, 0.18) * values
    return jnp.clip(values, min=-limit, max=limit).astype(kind)


def setup_inputs(seed: int = 0) -> dict:
    key_list = jax.random.split(jax.random.key(seed), 11)
    state = bell_draw(key_list[0], (STRIP_NODE_COUNT, TRANSVERSE_NODES, LEV * NF), 1.0, 6.0, ((0, 128), (1, 2), (2, 2)), jnp.float32)
    u_wind = bell_draw(key_list[1], (STRIP_NODE_COUNT, TRANSVERSE_NODES, LEV), 1.0, 4.0, ((0, 128), (1, 2), (2, 2)), jnp.float32)
    v_wind = bell_draw(key_list[2], (STRIP_NODE_COUNT, TRANSVERSE_NODES, LEV), 1.0, 4.0, ((0, 128), (1, 2), (2, 2)), jnp.float32)
    mixing = draw_mixing(jax.random.fold_in(key_list[10], 71), 0)
    stretch_order = draw_stretch_order(jax.random.fold_in(key_list[10], 71), 0)
    remap_index = set_ends(jax.random.randint(key_list[5], (OCELLS, REMAP), 0, COLS), jax.random.fold_in(key_list[5], 1), 0, COLS - 1).astype(jnp.int32)
    remap_weight = jnp.clip(0.1 + 0.9 * jax.random.uniform(key_list[6], (OCELLS, REMAP), jnp.float32) ** shard_levels(key_list[6], (OCELLS, REMAP), ((0, 512),), -0.2, 0.2), 0.1, 1.0)
    land_sea = set_ends((jax.random.randint(key_list[7], (OCELLS,), 0, 3) < 2).astype(jnp.int32), jax.random.fold_in(key_list[7], 1), 0, 1)
    ocean_temp = bell_draw(key_list[8], (OLEV, OCELLS), 1.0, 6.0, ((1, 512),), jnp.float32)
    ocean_mixing = draw_ocean_mixing(jax.random.fold_in(key_list[10], 71), 0)
    return dict(state=state, u_wind=u_wind, v_wind=v_wind, mixing=mixing, stretch_order=stretch_order, remap_index=remap_index, remap_weight=remap_weight, land_sea=land_sea, ocean_temp=ocean_temp, ocean_mixing=ocean_mixing)


HIGH = lax.Precision.HIGHEST

def gll_derivative():
    nodes = np.array([-1.0, -1.0 / math.sqrt(5.0), 1.0 / math.sqrt(5.0), 1.0])
    count = nodes.shape[0]
    bary = np.ones(count)
    for j in range(count):
        for k in range(count):
            if k != j:
                bary[j] = bary[j] / (nodes[j] - nodes[k])
    table = np.zeros((count, count))
    for i in range(count):
        for j in range(count):
            if i != j:
                table[i, j] = bary[j] / bary[i] / (nodes[i] - nodes[j])
        table[i, i] = -np.sum(table[i])
    return table.astype(np.float32)

def substep(field, u_rep, v_rep, deriv_table):
    lengthwise_extent, transverse_extent, chans = field.shape
    along_x = field.reshape(lengthwise_extent // NP, NP, transverse_extent, chans)
    diff_x = jnp.einsum('ij,ejyc->eiyc', deriv_table, along_x, precision=HIGH).reshape(field.shape)
    along_y = field.reshape(lengthwise_extent, transverse_extent // NP, NP, chans)
    diff_y = jnp.einsum('ij,xejc->xeic', deriv_table, along_y, precision=HIGH).reshape(field.shape)
    field = field - 0.1 * (u_rep * diff_x + v_rep * diff_y)
    blocks = field.reshape(lengthwise_extent // NP, NP, transverse_extent, chans)
    lead_row = blocks[:, 0]
    tail_row = blocks[:, NP - 1]
    average = 0.5 * (tail_row + jnp.roll(lead_row, -1, axis=0))
    blocks = blocks.at[:, NP - 1].set(average).at[:, 0].set(jnp.roll(average, 1, axis=0))
    field = blocks.reshape(field.shape)
    blocks = field.reshape(lengthwise_extent, transverse_extent // NP, NP, chans)
    lead_row = blocks[:, :, 0]
    tail_row = blocks[:, :, NP - 1]
    average = 0.5 * (tail_row[:, :-1] + lead_row[:, 1:])
    blocks = blocks.at[:, :-1, NP - 1].set(average).at[:, 1:, 0].set(average)
    return blocks.reshape(field.shape)

def physics(stretch, mixing):
    rows = stretch.shape[0]
    cube = stretch.reshape(rows, LEV, NF)
    mixed = jnp.einsum('kj,cjf->ckf', mixing, cube, precision=HIGH)
    temper = mixed[:, :, 0]
    vapour = mixed[:, :, 2]
    condense = jnp.maximum(vapour - 0.5 * jnp.exp(0.3 * temper), 0.0)
    mixed = mixed.at[:, :, 0].set(temper + 0.5 * condense).at[:, :, 2].set(vapour - condense)
    return (mixed.reshape(rows, LEV * NF), condense)

def reference(state, u_wind, v_wind, mixing, stretch_order, remap_index, remap_weight, land_sea, ocean_temp, ocean_mixing):
    deriv_table = jnp.asarray(gll_derivative())
    u_rep = jnp.repeat(u_wind, NF, axis=2)
    v_rep = jnp.repeat(v_wind, NF, axis=2)
    field = state
    for turn in range(2):
        field = substep(field, u_rep, v_rep, deriv_table)
    order_table = stretch_order.reshape(N_SEC, N_BLK, COLS)
    rows_all = jnp.arange(N_SEC * N_BLK * COLS, dtype=jnp.int32)
    inner = rows_all % STRETCH
    lev_part = rows_all // STRETCH % N_LEV
    blk_dest = rows_all // (STRETCH * N_LEV) % N_BLK
    sec_part = rows_all // (STRETCH * N_LEV * N_BLK)
    joined = lev_part * STRETCH + inner
    source = joined // SHARE
    offset = joined % SHARE
    local_col = order_table[sec_part, source, blk_dest * SHARE + offset]
    glob_col = (source * XPTS + local_col // YPTS) * TRANSVERSE_NODES + sec_part * YPTS + local_col % YPTS
    flat = field.reshape(STRIP_NODE_COUNT * TRANSVERSE_NODES, LEV * NF)
    stretch = flat[glob_col]
    advanced_segment_block, parameterized_rate_per_line = physics(stretch, mixing)
    flat_new = jnp.zeros_like(flat).at[glob_col].set(advanced_segment_block)
    advanced_model_quantities = flat_new.reshape(STRIP_NODE_COUNT, TRANSVERSE_NODES, LEV * NF)
    cube = flat_new.reshape(STRIP_NODE_COUNT * TRANSVERSE_NODES, LEV, NF)
    level_weight = (1.0 + jnp.arange(LEV, dtype=jnp.float32) / LEV) / math.sqrt(LEV)
    heat = lax.optimization_barrier(jnp.sum(cube[:, :, 0] * level_weight, axis=1))
    moist = lax.optimization_barrier(jnp.sum(cube[:, :, 2] * level_weight, axis=1))
    cells = jnp.arange(OCELLS, dtype=jnp.int32)
    owner = cells // OC
    blk_part = owner // N_LEV % N_BLK
    sec_cell = owner // (N_LEV * N_BLK)
    counterpart_device = 1 - sec_cell
    destination_entries = (blk_part[:, None] * XPTS + remap_index // YPTS) * TRANSVERSE_NODES + counterpart_device[:, None] * YPTS + remap_index % YPTS
    sea = land_sea.astype(jnp.float32)
    forcing = sea * lax.optimization_barrier(jnp.sum(remap_weight * (0.5 * heat[destination_entries] + 0.5 * moist[destination_entries]), axis=1))
    lifted = ocean_temp.at[0].set(ocean_temp[0] + forcing)
    refreshed_sea_depth_curves = jnp.dot(ocean_mixing, lifted, precision=HIGH, preferred_element_type=jnp.float32)
    surface = refreshed_sea_depth_curves[0]
    broadcast_entries = (remap_weight * (sea * surface)[:, None]).reshape(-1)
    skin_heat_linear_vector = jax.ops.segment_sum(broadcast_entries, destination_entries.reshape(-1), num_segments=STRIP_NODE_COUNT * TRANSVERSE_NODES)
    return (advanced_model_quantities, parameterized_rate_per_line, advanced_segment_block, refreshed_sea_depth_curves, skin_heat_linear_vector.reshape(STRIP_NODE_COUNT, TRANSVERSE_NODES))
```

```python
import functools
import math

import jax
import jax.numpy as jnp
import numpy as np
from jax import lax
from jax.experimental import pallas as pl
from jax.experimental.pallas import tpu as pltpu
from jax.sharding import PartitionSpec as P

NP = 4
LEV = 128
NF = 12
NX, NY = 8, 16
COLS = NX * NY
HL = 64
CH = HL * NF
NBLK = 128
LANES = 128
NQ = CH // LANES
F32 = jnp.float32
BF16 = jnp.bfloat16
HIGH = lax.Precision.HIGHEST
MESH = pl.DeviceIdType.MESH


def gll_derivative():
    nodes = np.array([-1.0, -1.0 / math.sqrt(5.0), 1.0 / math.sqrt(5.0), 1.0])
    count = nodes.shape[0]
    bary = np.ones(count)
    for j in range(count):
        for k in range(count):
            if k != j:
                bary[j] = bary[j] / (nodes[j] - nodes[k])
    table = np.zeros((count, count))
    for i in range(count):
        for j in range(count):
            if i != j:
                table[i, j] = bary[j] / bary[i] / (nodes[i] - nodes[j])
        table[i, i] = -np.sum(table[i])
    return table.astype(np.float32)


def iota(shape, dim):
    return lax.broadcasted_iota(jnp.int32, shape, dim)


def split2(x):
    hi = x.astype(BF16)
    lo = (x - hi.astype(F32)).astype(BF16)
    return hi, lo


def dot(a, b):
    return jnp.dot(a, b, preferred_element_type=F32)


def dot3(a, b_hi, b_lo):
    hi, lo = split2(a)
    return dot(hi, b_hi) + dot(lo, b_hi) + dot(hi, b_lo)


def remote(src, dst, send, recv, device):
    return pltpu.make_async_remote_copy(
        src_ref=src, dst_ref=dst, send_sem=send, recv_sem=recv,
        device_id=device, device_id_type=MESH,
    )


def row(ref, r):
    return ref.at[pl.ds(r, 1)]


def advect(field_ref, uw_ref, vw_ref, out_ref, table):
    y8 = iota((8, LANES), 0)
    at = lax.rem(y8, NP)
    coefs = {}
    for d in range(-3, 4):
        c = jnp.zeros((8, LANES), F32)
        for i in range(NP):
            if 0 <= i + d < NP:
                c = jnp.where(at == i, F32(table[i, i + d]), c)
        coefs[d] = c[None]
    for q in range(NQ):
        lanes = slice(q * LANES, (q + 1) * LANES)
        for e in range(2):
            rows = slice(e * 64, (e + 1) * 64)
            f = field_ref[rows, lanes].reshape(NP, NY, LANES)
            dx = []
            for i in range(NP):
                acc = F32(table[i, 0]) * f[0]
                for j in range(1, NP):
                    acc = acc + F32(table[i, j]) * f[j]
                dx.append(acc[None])
            dx = jnp.concatenate(dx, axis=0).reshape(64, LANES)
            f8 = f.reshape(8, 8, LANES)
            dy = coefs[0] * f8
            for d in (-3, -2, -1, 1, 2, 3):
                dy = dy + coefs[d] * pltpu.roll(f8, (-d) % 8, axis=1)
            dy = dy.reshape(64, LANES)
            out_ref[rows, lanes] = f.reshape(64, LANES) - (
                uw_ref[rows, :] * dx + vw_ref[rows, :] * dy
            )


def average(a_ref, x_from_left, x_from_right, edge_ref, cor_l, cor_r, out_ref, s):
    y = iota((NY, LANES), 0)
    i = lax.rem(y, NP)
    at_edge = ((y == NY - 1) & (s == 0)) | ((y == 0) & (s == 1))
    closed = ((y == NY - 1) & (s == 1)) | ((y == 0) & (s == 0))
    inside = ((i == 0) | (i == NP - 1)) & jnp.logical_not(closed)
    for q in range(NQ):
        lanes = slice(q * LANES, (q + 1) * LANES)
        a = [a_ref[x * NY:(x + 1) * NY, lanes] for x in range(NX)]
        e = edge_ref[:, lanes]
        e = [e[x:x + 1] for x in range(NX)]
        a[0] = 0.5 * (a[0] + x_from_left[:, lanes])
        a[7] = 0.5 * (a[7] + x_from_right[:, lanes])
        a[3] = a[4] = 0.5 * (a[3] + a[4])
        e[0] = 0.5 * (e[0] + cor_l[0:1, lanes])
        e[7] = 0.5 * (e[7] + cor_r[0:1, lanes])
        e[3] = e[4] = 0.5 * (e[3] + e[4])
        for x in range(NX):
            f = a[x]
            up = pltpu.roll(f, NY - 1, axis=0)
            dn = pltpu.roll(f, 1, axis=0)
            nb = jnp.where(i == NP - 1, up, dn)
            nb = jnp.where(at_edge, jnp.broadcast_to(e[x], (NY, LANES)), nb)
            out_ref[x * NY:(x + 1) * NY, lanes] = jnp.where(inside, 0.5 * (f + nb), f)


def window_kernel(
    state_ref, u_ref, v_ref, mixing_ref, order_ref, index_ref, weight_ref, sea_ref, temp_ref, omix_ref,
    adv_ref, rate_ref, rows_ref, curves_ref, sst_ref,
    perm, perm_t, uw, vw, field, adv1, adv2, edge1, edge2, xl, xr, ye, cl, cr,
    gone, came, tv, flux_out, flux_in, sst_out, sst_in, back, home, mixed, spare,
    halo_send, halo_recv, tv_send, tv_recv, flux_send, flux_recv, sst_send, sst_recv,
    go_send, go_recv, back_send, back_recv,
):
    s, b, l = lax.axis_index("sec"), lax.axis_index("blk"), lax.axis_index("lev")
    table = gll_derivative()
    left, right = lax.rem(b + NBLK - 1, NBLK), lax.rem(b + 1, NBLK)
    half = b // 64
    low = lax.rem(b, 64)
    own = l == half

    barrier = pltpu.get_barrier_semaphore()

    def greet(device):
        pl.semaphore_signal(barrier, inc=1, device_id=device, device_id_type=MESH)

    near = [(s, left, l), (s, right, l), (1 - s, b, l), (1 - s, left, l), (1 - s, right, l), (s, b, 1 - l), (1 - s, b, 1 - l)]
    for device in near:
        greet(device)

    def greet_sources(i, carry):
        j = l * 64 + lax.rem(low + i, 64)
        greet((s, j, 0))
        greet((s, j, 1))
        return carry

    lax.fori_loop(0, 64, greet_sources, 0, unroll=8)

    for q in range(NQ):
        wide = (CH, LANES)
        to = iota(wide, 1) + q * LANES
        perm[:, q * LANES:(q + 1) * LANES] = jnp.where(
            iota(wide, 0) == lax.rem(to, HL) * NF + to // HL, F32(1), F32(0)
        ).astype(BF16)
        perm_t[:, q * LANES:(q + 1) * LANES] = jnp.where(
            to == lax.rem(iota(wide, 0), HL) * NF + iota(wide, 0) // HL, F32(1), F32(0)
        ).astype(BF16)
    hi, lo = split2(state_ref[...])
    field[...] = dot(hi, perm[...]) + dot(lo, perm[...])
    for ref, wind in ((uw, u_ref), (vw, v_ref)):
        w = F32(0.1) * wind[...]
        ref[...] = jnp.concatenate([w, w], axis=1)

    square = (COLS, COLS)
    hot_t = jnp.where(iota(square, 0) == order_ref[...], F32(1), F32(0))
    hot = hot_t.T.astype(BF16)
    hot_t = hot_t.astype(BF16)

    mt = mixing_ref[...].T
    lane = iota((HL, LANES), 1)
    blocks = []
    for li in range(2):
        part = mt[li * HL:(li + 1) * HL]
        turned = pltpu.roll(part, HL, axis=1)
        zero = jnp.zeros_like(part)
        blocks.append(jnp.concatenate([jnp.where(lane < HL, part, zero), jnp.where(lane < HL, turned, zero)], axis=1))
        blocks.append(jnp.concatenate([jnp.where(lane < HL, zero, turned), jnp.where(lane < HL, zero, part)], axis=1))
    pair_hi, pair_lo = split2(jnp.concatenate(blocks, axis=0))

    sea = sea_ref[...].astype(F32)
    weigh = jnp.zeros(square, F32)
    for m in range(4):
        weigh = weigh + jnp.where(iota(square, 0) == index_ref[m:m + 1, :], weight_ref[m:m + 1, :], F32(0))
    calm = jnp.dot(omix_ref[...], temp_ref[...], precision=HIGH, preferred_element_type=F32)

    advect(field, uw, vw, adv1, table)
    pl.semaphore_wait(barrier, len(near) + 128)

    sends = []
    for turn, (a, edge) in enumerate(((adv1, edge1), (adv2, edge2))):
        if turn == 1:
            advect(field, uw, vw, a, table)
        for x in range(NX):
            bottom, top = a[x * NY:x * NY + 1, :], a[(x + 1) * NY - 1:(x + 1) * NY, :]
            edge[x:x + 1, :] = jnp.where(s == 0, top, bottom)
        parts = (
            (a.at[pl.ds(0, NY)], xr.at[turn], (s, left, l)),
            (a.at[pl.ds(COLS - NY, NY)], xl.at[turn], (s, right, l)),
            (edge, ye.at[turn], (1 - s, b, l)),
            (row(edge, 0), cr.at[turn], (1 - s, left, l)),
            (row(edge, NX - 1), cl.at[turn], (1 - s, right, l)),
        )
        copies = [
            remote(src, dst, halo_send.at[turn, i], halo_recv.at[turn, i], device)
            for i, (src, dst, device) in enumerate(parts)
        ]
        for c in copies:
            c.start()
        for c in copies:
            c.wait_recv()
        sends += copies
        average(a, xl.at[turn], xr.at[turn], ye.at[turn], cl.at[turn], cr.at[turn], field, s)

    lane128 = iota((COLS, LANES), 1)
    tv[pl.ds(l, 1)] = jnp.where(
        lane128 < HL, field[:, 0:LANES], pltpu.roll(field[:, LANES:2 * LANES], HL, axis=1)
    )[None]
    tv_copy = remote(tv.at[l], tv.at[l], tv_send, tv_recv, (s, b, 1 - l))
    tv_copy.start()
    sends.append(tv_copy)

    hi, lo = split2(field[...])
    gone[...] = dot(hot, hi) + dot(hot, lo)
    slot = l * 64 + low
    bx, by, bz = b // 32, lax.rem(b // 4, 8), lax.rem(b, 4)

    def send_column(t, carry):
        dz, dx, dy = lax.rem(t, 4), lax.rem(t // 4, 4), t // 16
        p = lax.rem(bx + dx, 4) * 32 + lax.rem(by + dy, 8) * 4 + lax.rem(bz + dz, 4)
        remote(row(gone, p), row(came, slot), go_send, go_recv, (s, p, half)).start()
        return carry

    lax.fori_loop(1, 128, send_column, 0, unroll=8)

    @pl.when(own)
    def _():
        pltpu.make_async_copy(row(gone, b), row(came, slot), go_recv).start()
        pltpu.make_async_copy(row(gone, b), spare.at[0], go_send).start()

    @pl.when(jnp.logical_not(own))
    def _():
        send_column(0, 0)

    tv_copy.wait_recv()
    whole = jnp.concatenate([tv[0], tv[1]], axis=1)
    both = dot3(whole, pair_hi, pair_lo)
    level = lax.rem(lane128, HL)
    total = jnp.zeros((COLS, LANES), F32)
    for lo_ in range(2):
        part = both[:, lo_ * LANES:(lo_ + 1) * LANES]
        vapour = pltpu.roll(part, HL, axis=1)
        condense = jnp.maximum(vapour - 0.5 * jnp.exp(0.3 * part), 0.0)
        heat = part + 0.5 * condense
        moist = vapour - condense
        w = (1.0 + (level + lo_ * HL).astype(F32) / LEV) / math.sqrt(LEV)
        total = total + jnp.where(lane128 < HL, w * (0.5 * heat + 0.5 * moist), 0.0)
    flux = jnp.sum(total.T, axis=0, keepdims=True)
    flux_out[...] = jnp.broadcast_to(flux, (8, LANES))
    flux_copy = remote(flux_out, flux_in, flux_send, flux_recv, (1 - s, b, l))
    flux_copy.start()
    sends.append(flux_copy)

    flux_copy.wait_recv()
    forcing = jnp.dot(flux_in[...], weigh, precision=HIGH, preferred_element_type=F32)
    forcing = sea * forcing[0:1]
    curves = calm + omix_ref[:, 0:1] * forcing
    curves_ref[...] = curves
    entry = jnp.broadcast_to(sea * curves[0:1], (8, LANES))
    sst_out[...] = lax.dot_general(
        entry, weigh, (((1,), (1,)), ((), ())), precision=HIGH, preferred_element_type=F32
    )
    sst_copies = [
        remote(sst_out, sst_in.at[l], sst_send.at[k], sst_recv.at[l], (1 - s, b, k)) for k in range(2)
    ]
    for c in sst_copies:
        c.start()

    pltpu.make_async_copy(came, came, go_recv).wait()
    wide = jnp.concatenate(
        [
            jnp.concatenate([came[0:64, q * LANES:(q + 1) * LANES], came[64:128, q * LANES:(q + 1) * LANES]], axis=1)
            for q in range(NQ)
        ],
        axis=0,
    )
    done = dot3(wide, pair_hi, pair_lo)
    for q in range(NQ):
        for h in range(2):
            mixed[h * 64:(h + 1) * 64, q * LANES:(q + 1) * LANES] = done[
                q * 64:(q + 1) * 64, h * LANES:(h + 1) * LANES
            ]
    temper = mixed[:, 0:LANES]
    vapour = mixed[:, LANES:2 * LANES]
    condense = jnp.maximum(vapour - 0.5 * jnp.exp(0.3 * temper), 0.0)
    mixed[:, 0:LANES] = jnp.where(lane128 < HL, temper + 0.5 * condense, temper)
    mixed[:, LANES:2 * LANES] = jnp.where(lane128 < HL, vapour - condense, vapour)
    rate_ref[...] = jnp.where(lane < HL, condense[0:64], pltpu.roll(condense[64:128], HL, axis=1))
    hi, lo = split2(mixed[...])
    back[...] = dot(hi, perm_t[...]) + dot(lo, perm_t[...])

    def send_row(t, carry):
        dl, dz, dx, dy = lax.rem(t, 2), lax.rem(t // 2, 4), lax.rem(t // 8, 2), t // 16
        i = lax.rem(lax.rem(bx, 2) + dx, 2) * 32 + lax.rem(by + dy, 8) * 4 + lax.rem(bz + dz, 4)
        k = lax.rem(l + dl, 2)
        remote(row(back, k * 64 + i), row(home, b), back_send, back_recv, (s, l * 64 + i, k)).start()
        return carry

    lax.fori_loop(1, 128, send_row, 0, unroll=8)

    @pl.when(own)
    def _():
        pltpu.make_async_copy(row(back, slot), row(home, b), back_recv).start()
        pltpu.make_async_copy(row(back, slot), spare.at[1], back_send).start()

    @pl.when(jnp.logical_not(own))
    def _():
        send_row(0, 0)

    for h in range(2):
        rows_ref[:, h * CH:(h + 1) * CH] = back[h * 64:(h + 1) * 64, :]

    for k in range(2):
        remote(sst_out, sst_in.at[k], sst_send.at[k], sst_recv.at[k], (1 - s, b, k)).wait_recv()
    surface = sst_in[0] + sst_in[1]
    col = iota((8, LANES), 1)
    surface = jnp.where(col // NY == iota((8, LANES), 0), surface, 0.0)
    pick = jnp.where(lax.rem(iota((COLS, NY), 0), NY) == iota((COLS, NY), 1), F32(1), F32(0))
    sst_ref[...] = jnp.dot(surface, pick, precision=HIGH, preferred_element_type=F32)

    pltpu.make_async_copy(home, home, back_recv).wait()
    hi, lo = split2(home[...])
    adv_ref[...] = dot(hot_t, hi) + dot(hot_t, lo)

    pltpu.make_async_copy(gone, came, go_send).wait()
    pltpu.make_async_copy(back, home, back_send).wait()
    for c in sends:
        c.wait_send()
    for c in sst_copies:
        c.wait_send()


def on_device(
    state, u_wind, v_wind, mixing, stretch_order, remap_index, remap_weight, land_sea, ocean_temp, ocean_mixing,
):
    vmem = pl.BlockSpec(memory_space=pltpu.VMEM)
    dma = pltpu.SemaphoreType.DMA
    big = pltpu.VMEM((COLS, CH), F32)
    scratch = [
        pltpu.VMEM((CH, CH), BF16), pltpu.VMEM((CH, CH), BF16),
        pltpu.VMEM((COLS, LANES), F32), pltpu.VMEM((COLS, LANES), F32),
        big, big, big,
        pltpu.VMEM((NX, CH), F32), pltpu.VMEM((NX, CH), F32),
        pltpu.VMEM((2, NY, CH), F32), pltpu.VMEM((2, NY, CH), F32),
        pltpu.VMEM((2, NX, CH), F32),
        pltpu.VMEM((2, 1, CH), F32), pltpu.VMEM((2, 1, CH), F32),
        big, big,
        pltpu.VMEM((2, COLS, LANES), F32),
        pltpu.VMEM((8, LANES), F32), pltpu.VMEM((8, LANES), F32),
        pltpu.VMEM((8, LANES), F32), pltpu.VMEM((2, 8, LANES), F32),
        big, big, big,
        pltpu.VMEM((2, 1, CH), F32),
        dma((2, 5)), dma((2, 5)), dma, dma, dma, dma, dma((2,)), dma((2,)),
        dma, dma, dma, dma,
    ]
    outs = pl.pallas_call(
        window_kernel,
        out_shape=[
            jax.ShapeDtypeStruct((COLS, CH), F32),
            jax.ShapeDtypeStruct((64, LEV), F32),
            jax.ShapeDtypeStruct((64, LEV * NF), F32),
            jax.ShapeDtypeStruct(ocean_temp.shape, F32),
            jax.ShapeDtypeStruct((NX, NY), F32),
        ],
        in_specs=[vmem] * 10,
        out_specs=[vmem] * 5,
        scratch_shapes=scratch,
        compiler_params=pltpu.CompilerParams(
            collective_id=0, has_side_effects=True, vmem_limit_bytes=48 * 2**20
        ),
        name="window",
    )(
        state.reshape(COLS, CH),
        u_wind.reshape(COLS, HL),
        v_wind.reshape(COLS, HL),
        mixing,
        stretch_order.reshape(1, COLS),
        remap_index.T,
        remap_weight.T,
        land_sea.reshape(1, COLS),
        ocean_temp,
        ocean_mixing,
    )
    return (outs[0].reshape(state.shape), *outs[1:])


def solution(mesh):
    placed = (
        P("blk", "sec", "lev"),
        P("blk", "sec", "lev"),
        P("blk", "sec", "lev"),
        P(),
        P(("sec", "blk")),
        P(("sec", "blk", "lev"), None),
        P(("sec", "blk", "lev"), None),
        P(("sec", "blk", "lev")),
        P(None, ("sec", "blk", "lev")),
        P(),
    )
    return jax.shard_map(
        on_device,
        mesh=mesh,
        in_specs=placed,
        out_specs=(
            P("blk", "sec", "lev"),
            P(("sec", "blk", "lev"), None),
            P(("sec", "blk", "lev"), None),
            P(None, ("sec", "blk", "lev")),
            P("blk", "sec"),
        ),
        check_vma=False,
    )
```

```python
import functools
import math

import jax
import jax.numpy as jnp
import numpy as np
from jax import lax
from jax.experimental import pallas as pl
from jax.experimental.pallas import tpu as pltpu
from jax.sharding import PartitionSpec as P

NP = 4
LEV = 128
NF = 12
NX, NY = 8, 16
COLS = NX * NY
HL = 64
CH = HL * NF
NBLK = 128
LANES = 128
NQ = CH // LANES
F32 = jnp.float32
BF16 = jnp.bfloat16
HIGH = lax.Precision.HIGHEST
MESH = pl.DeviceIdType.MESH


def gll_derivative():
    nodes = np.array([-1.0, -1.0 / math.sqrt(5.0), 1.0 / math.sqrt(5.0), 1.0])
    count = nodes.shape[0]
    bary = np.ones(count)
    for j in range(count):
        for k in range(count):
            if k != j:
                bary[j] = bary[j] / (nodes[j] - nodes[k])
    table = np.zeros((count, count))
    for i in range(count):
        for j in range(count):
            if i != j:
                table[i, j] = bary[j] / bary[i] / (nodes[i] - nodes[j])
        table[i, i] = -np.sum(table[i])
    return table.astype(np.float32)


def iota(shape, dim):
    return lax.broadcasted_iota(jnp.int32, shape, dim)


def split2(x):
    hi = x.astype(BF16)
    lo = (x - hi.astype(F32)).astype(BF16)
    return hi, lo


def dot(a, b):
    return jnp.dot(a, b, preferred_element_type=F32)


def dot3(a, b_hi, b_lo):
    hi, lo = split2(a)
    return dot(hi, b_hi) + dot(lo, b_hi) + dot(hi, b_lo)


def remote(src, dst, send, recv, device):
    return pltpu.make_async_remote_copy(
        src_ref=src, dst_ref=dst, send_sem=send, recv_sem=recv,
        device_id=device, device_id_type=MESH,
    )


def row(ref, r):
    return ref.at[pl.ds(r, 1)]


def advect(field_ref, uw_ref, vw_ref, out_ref, table):
    y8 = iota((8, LANES), 0)
    at = lax.rem(y8, NP)
    coefs = {}
    for d in range(-3, 4):
        c = jnp.zeros((8, LANES), F32)
        for i in range(NP):
            if 0 <= i + d < NP:
                c = jnp.where(at == i, F32(table[i, i + d]), c)
        coefs[d] = c[None]
    for q in range(NQ):
        lanes = slice(q * LANES, (q + 1) * LANES)
        for e in range(2):
            rows = slice(e * 64, (e + 1) * 64)
            f = field_ref[rows, lanes].reshape(NP, NY, LANES)
            dx = []
            for i in range(NP):
                acc = F32(table[i, 0]) * f[0]
                for j in range(1, NP):
                    acc = acc + F32(table[i, j]) * f[j]
                dx.append(acc[None])
            dx = jnp.concatenate(dx, axis=0).reshape(64, LANES)
            f8 = f.reshape(8, 8, LANES)
            dy = coefs[0] * f8
            for d in (-3, -2, -1, 1, 2, 3):
                dy = dy + coefs[d] * pltpu.roll(f8, (-d) % 8, axis=1)
            dy = dy.reshape(64, LANES)
            out_ref[rows, lanes] = f.reshape(64, LANES) - (
                uw_ref[rows, :] * dx + vw_ref[rows, :] * dy
            )


def average(a_ref, x_from_left, x_from_right, edge_ref, cor_l, cor_r, out_ref, s):
    y = iota((NY, LANES), 0)
    i = lax.rem(y, NP)
    at_edge = ((y == NY - 1) & (s == 0)) | ((y == 0) & (s == 1))
    closed = ((y == NY - 1) & (s == 1)) | ((y == 0) & (s == 0))
    inside = ((i == 0) | (i == NP - 1)) & jnp.logical_not(closed)
    for q in range(NQ):
        lanes = slice(q * LANES, (q + 1) * LANES)
        a = [a_ref[x * NY:(x + 1) * NY, lanes] for x in range(NX)]
        e = edge_ref[:, lanes]
        e = [e[x:x + 1] for x in range(NX)]
        a[0] = 0.5 * (a[0] + x_from_left[:, lanes])
        a[7] = 0.5 * (a[7] + x_from_right[:, lanes])
        a[3] = a[4] = 0.5 * (a[3] + a[4])
        e[0] = 0.5 * (e[0] + cor_l[0:1, lanes])
        e[7] = 0.5 * (e[7] + cor_r[0:1, lanes])
        e[3] = e[4] = 0.5 * (e[3] + e[4])
        for x in range(NX):
            f = a[x]
            up = pltpu.roll(f, NY - 1, axis=0)
            dn = pltpu.roll(f, 1, axis=0)
            nb = jnp.where(i == NP - 1, up, dn)
            nb = jnp.where(at_edge, jnp.broadcast_to(e[x], (NY, LANES)), nb)
            out_ref[x * NY:(x + 1) * NY, lanes] = jnp.where(inside, 0.5 * (f + nb), f)


def window_kernel(
    state_hbm, u_hbm, v_hbm, mixing_hbm, order_hbm, index_hbm, weight_hbm, sea_hbm, temp_hbm, omix_hbm,
    adv_hbm, rate_hbm, rows_hbm, curves_hbm, sst_hbm,
    state_ref, u_ref, v_ref, mixing_ref, order_ref, index_ref, weight_ref, sea_ref, temp_ref, omix_ref,
    adv_ref, rate_ref, rows_ref, curves_ref, sst_ref, in_sems, out_sems,
    perm, perm_t, uw, vw, field, adv1, adv2, edge1, edge2, xl, xr, ye, cl, cr,
    gone, came, tv, flux_out, flux_in, sst_out, sst_in, back, home, mixed, spare,
    halo_send, halo_recv, tv_send, tv_recv, flux_send, flux_recv, sst_send, sst_recv,
    go_send, go_recv, back_send, back_recv,
    mid, mid2, plane, mid_send, mid_recv, stay_sem, home_send, home_recv, home_stay,
):
    s, b, l = lax.axis_index("sec"), lax.axis_index("blk"), lax.axis_index("lev")
    table = gll_derivative()
    left, right = lax.rem(b + NBLK - 1, NBLK), lax.rem(b + 1, NBLK)

    loads = [
        pltpu.make_async_copy(src, dst, in_sems.at[i])
        for i, (src, dst) in enumerate((
            (state_hbm, state_ref), (u_hbm, u_ref), (v_hbm, v_ref), (order_hbm, order_ref), (mixing_hbm, mixing_ref),
            (index_hbm, index_ref), (weight_hbm, weight_ref), (sea_hbm, sea_ref), (temp_hbm, temp_ref), (omix_hbm, omix_ref),
        ))
    ]
    for c in loads:
        c.start()

    barrier = pltpu.get_barrier_semaphore()

    def greet(device):
        pl.semaphore_signal(barrier, inc=1, device_id=device, device_id_type=MESH)

    bx, by, bz = b // 32, lax.rem(b // 4, 8), lax.rem(b, 4)
    pair = by // 2
    along_x = [(s, lax.rem(bx + d, 4) * 32 + lax.rem(b, 32), l) for d in range(1, 4)]
    along_y = [(s, bx * 32 + lax.rem(by + d, 8) * 4 + bz, l) for d in range(1, 8)]
    along_z = [(s, bx * 32 + by * 4 + lax.rem(bz + d, 4), l) for d in range(1, 4)]
    along_z += [(s, bx * 32 + by * 4 + lax.rem(bz + d, 4), 1 - l) for d in range(4)]
    near = [(s, left, l), (s, right, l), (1 - s, b, l), (1 - s, left, l), (1 - s, right, l), (1 - s, b, 1 - l)]
    near += along_x + along_z + along_y
    for device in near:
        greet(device)

    for q in range(NQ):
        wide = (CH, LANES)
        to = iota(wide, 1) + q * LANES
        perm[:, q * LANES:(q + 1) * LANES] = jnp.where(
            iota(wide, 0) == lax.rem(to, HL) * NF + to // HL, F32(1), F32(0)
        ).astype(BF16)
        perm_t[:, q * LANES:(q + 1) * LANES] = jnp.where(
            to == lax.rem(iota(wide, 0), HL) * NF + iota(wide, 0) // HL, F32(1), F32(0)
        ).astype(BF16)
    for c in loads[:3]:
        c.wait()
    hi, lo = split2(state_ref[...])
    field[...] = dot(hi, perm[...]) + dot(lo, perm[...])
    for ref, wind in ((uw, u_ref), (vw, v_ref)):
        w = F32(0.1) * wind[...]
        ref[...] = jnp.concatenate([w, w], axis=1)

    for c in loads[3:]:
        c.wait()

    square = (COLS, COLS)
    hot_t = jnp.where(iota(square, 0) == order_ref[...], F32(1), F32(0))
    hot = hot_t.T.astype(BF16)
    hot_t = hot_t.astype(BF16)

    mt = mixing_ref[...].T
    lane = iota((HL, LANES), 1)
    blocks = []
    for li in range(2):
        part = mt[li * HL:(li + 1) * HL]
        turned = pltpu.roll(part, HL, axis=1)
        zero = jnp.zeros_like(part)
        blocks.append(jnp.concatenate([jnp.where(lane < HL, part, zero), jnp.where(lane < HL, turned, zero)], axis=1))
        blocks.append(jnp.concatenate([jnp.where(lane < HL, zero, turned), jnp.where(lane < HL, zero, part)], axis=1))
    pair_hi, pair_lo = split2(jnp.concatenate(blocks, axis=0))

    sea = sea_ref[...].astype(F32)
    weigh = jnp.zeros(square, F32)
    for m in range(4):
        weigh = weigh + jnp.where(iota(square, 0) == index_ref[m:m + 1, :], weight_ref[m:m + 1, :], F32(0))
    calm = jnp.dot(omix_ref[...], temp_ref[...], precision=HIGH, preferred_element_type=F32)

    advect(field, uw, vw, adv1, table)
    pl.semaphore_wait(barrier, len(near))
    for device in along_y:
        pl.semaphore_signal(plane, inc=1, device_id=device, device_id_type=MESH)

    sends = []
    for turn, (a, edge) in enumerate(((adv1, edge1), (adv2, edge2))):
        if turn == 1:
            advect(field, uw, vw, a, table)
        for x in range(NX):
            bottom, top = a[x * NY:x * NY + 1, :], a[(x + 1) * NY - 1:(x + 1) * NY, :]
            edge[x:x + 1, :] = jnp.where(s == 0, top, bottom)
        parts = (
            (a.at[pl.ds(0, NY)], xr.at[turn], (s, left, l)),
            (a.at[pl.ds(COLS - NY, NY)], xl.at[turn], (s, right, l)),
            (edge, ye.at[turn], (1 - s, b, l)),
            (row(edge, 0), cr.at[turn], (1 - s, left, l)),
            (row(edge, NX - 1), cl.at[turn], (1 - s, right, l)),
        )
        copies = [
            remote(src, dst, halo_send.at[turn, i], halo_recv.at[turn, i], device)
            for i, (src, dst, device) in enumerate(parts)
        ]
        for c in copies:
            c.start()
        for c in copies:
            c.wait_recv()
        sends += copies
        average(a, xl.at[turn], xr.at[turn], ye.at[turn], cl.at[turn], cr.at[turn], field, s)

    lane128 = iota((COLS, LANES), 1)
    hi, lo = split2(field[...])
    gone[...] = dot(hot, hi) + dot(hot, lo)
    here = by * 4 + bz

    def rows_of(turned):
        return pl.ds(pl.multiple_of(turned * 8, 8), 8)

    def block(x, turned):
        return pl.ds(pl.multiple_of(x * 32 + turned * 8, 8), 8)

    def in_pair(c, j):
        y = lax.rem(pair + c, 4) * 2 + lax.rem(by + j // 8, 2)
        return y * 4 + lax.rem(bz + j // 2, 4), lax.rem(l + j, 2)

    across = []
    for c in range(4):
        turned = lax.rem(pair + c, 4)
        for d in range(3):
            copy = remote(
                gone.at[block(lax.rem(bx + d + 1, 4), turned)], mid.at[bx, rows_of(turned)],
                mid_send.at[c, d], mid_recv.at[c, d], along_x[d],
            )
            copy.start()
            across.append(copy)
    stay = pltpu.make_async_copy(gone.at[pl.ds(pl.multiple_of(bx * 32, 32), 32)], mid.at[bx], stay_sem)
    stay.start()
    sends += across

    tv[pl.ds(l, 1)] = jnp.where(
        lane128 < HL, field[:, 0:LANES], pltpu.roll(field[:, LANES:2 * LANES], HL, axis=1)
    )[None]
    tv_copy = remote(tv.at[l], tv.at[l], tv_send, tv_recv, (s, b, 1 - l))
    tv_copy.start()
    sends.append(tv_copy)

    pl.semaphore_wait(plane, len(along_y))
    stay.wait()

    def both_x(ref, h, place):
        return ref.at[pl.ds(h * 2, 2), pl.ds(place, 1)]

    for c in range(4):
        for d in range(3):
            across[c * 3 + d].wait_recv()

        def send_columns(j, carry, c=c):
            place, h = in_pair(c, j)
            remote(
                both_x(mid, h, place), both_x(came, l, here), go_send, go_recv, (s, bx * 32 + place, h)
            ).start()
            return carry

        lax.fori_loop(1 if c == 0 else 0, 16, send_columns, 0, unroll=True)
        if c == 0:
            pltpu.make_async_copy(both_x(mid, l, here), both_x(came, l, here), go_recv).start()
            pltpu.make_async_copy(both_x(mid, l, here), spare.at[0], go_send).start()

    pltpu.make_async_copy(came, came, go_recv).wait()
    wide = jnp.concatenate(
        [
            jnp.concatenate(
                [came[h * 2:h * 2 + 2, :, q * LANES:(q + 1) * LANES].reshape(64, LANES) for h in range(2)], axis=1
            )
            for q in range(NQ)
        ],
        axis=0,
    )
    done = dot3(wide, pair_hi, pair_lo)
    for q in range(NQ):
        for h in range(2):
            mixed[h * 64:(h + 1) * 64, q * LANES:(q + 1) * LANES] = done[
                q * 64:(q + 1) * 64, h * LANES:(h + 1) * LANES
            ]
    temper = mixed[:, 0:LANES]
    vapour = mixed[:, LANES:2 * LANES]
    condense = jnp.maximum(vapour - 0.5 * jnp.exp(0.3 * temper), 0.0)
    mixed[:, 0:LANES] = jnp.where(lane128 < HL, temper + 0.5 * condense, temper)
    mixed[:, LANES:2 * LANES] = jnp.where(lane128 < HL, vapour - condense, vapour)
    rate_ref[...] = jnp.where(lane < HL, condense[0:64], pltpu.roll(condense[64:128], HL, axis=1))
    hi, lo = split2(mixed[...])
    back[...] = (dot(hi, perm_t[...]) + dot(lo, perm_t[...])).reshape(4, 32, CH)

    for c in range(4):

        def send_rows(j, carry, c=c):
            place, k = in_pair(c, j)
            remote(
                both_x(back, k, place), both_x(mid2, l, here), back_send, back_recv.at[c], (s, bx * 32 + place, k)
            ).start()
            return carry

        lax.fori_loop(1 if c == 0 else 0, 16, send_rows, 0, unroll=True)
        if c == 0:
            pltpu.make_async_copy(both_x(back, l, here), both_x(mid2, l, here), back_recv.at[0]).start()
            pltpu.make_async_copy(both_x(back, l, here), spare.at[1], back_send).start()

    tv_copy.wait_recv()
    whole = jnp.concatenate([tv[0], tv[1]], axis=1)
    both = dot3(whole, pair_hi, pair_lo)
    level = lax.rem(lane128, HL)
    total = jnp.zeros((COLS, LANES), F32)
    for lo_ in range(2):
        part = both[:, lo_ * LANES:(lo_ + 1) * LANES]
        vapour = pltpu.roll(part, HL, axis=1)
        condense = jnp.maximum(vapour - 0.5 * jnp.exp(0.3 * part), 0.0)
        heat = part + 0.5 * condense
        moist = vapour - condense
        w = (1.0 + (level + lo_ * HL).astype(F32) / LEV) / math.sqrt(LEV)
        total = total + jnp.where(lane128 < HL, w * (0.5 * heat + 0.5 * moist), 0.0)
    flux = jnp.sum(total.T, axis=0, keepdims=True)
    flux_out[...] = jnp.broadcast_to(flux, (8, LANES))
    flux_copy = remote(flux_out, flux_in, flux_send, flux_recv, (1 - s, b, l))
    flux_copy.start()
    sends.append(flux_copy)

    def pass_rows(c):
        turned = lax.rem(pair + 4 - c, 4)
        arrived = mid2.at[:, rows_of(turned)]
        pltpu.make_async_copy(arrived, arrived, back_recv.at[c]).wait()
        for d in range(3):
            copy = remote(
                mid2.at[lax.rem(bx + d + 1, 4), rows_of(turned)], home.at[block(bx, turned)],
                home_send.at[c, d], home_recv.at[c, d], along_x[d],
            )
            copy.start()
            last.append(copy)
        copy = pltpu.make_async_copy(mid2.at[bx, rows_of(turned)], home.at[block(bx, turned)], home_stay.at[c])
        copy.start()
        stays.append(copy)

    last, stays = [], []
    pass_rows(0)
    pass_rows(1)

    flux_copy.wait_recv()
    forcing = jnp.dot(flux_in[...], weigh, precision=HIGH, preferred_element_type=F32)
    forcing = sea * forcing[0:1]
    curves = calm + omix_ref[:, 0:1] * forcing
    curves_ref[...] = curves
    entry = jnp.broadcast_to(sea * curves[0:1], (8, LANES))
    sst_out[...] = lax.dot_general(
        entry, weigh, (((1,), (1,)), ((), ())), precision=HIGH, preferred_element_type=F32
    )
    sst_copies = [
        remote(sst_out, sst_in.at[l], sst_send.at[k], sst_recv.at[l], (1 - s, b, k)) for k in range(2)
    ]
    for c in sst_copies:
        c.start()

    pass_rows(2)
    pass_rows(3)
    for h in range(2):
        rows_ref[:, h * CH:(h + 1) * CH] = back[h * 2:h * 2 + 2].reshape(64, CH)

    def store(i, src, dst):
        c = pltpu.make_async_copy(src, dst, out_sems.at[i])
        c.start()
        return c

    stores = [store(0, rate_ref, rate_hbm), store(1, rows_ref, rows_hbm), store(2, curves_ref, curves_hbm)]

    for c in stays:
        c.wait()
    for c in last:
        c.wait_recv()
    sends += last
    hi, lo = split2(home[...])
    adv_ref[...] = dot(hot_t, hi) + dot(hot_t, lo)

    stores.append(store(3, adv_ref, adv_hbm))

    for k in range(2):
        remote(sst_out, sst_in.at[k], sst_send.at[k], sst_recv.at[k], (1 - s, b, k)).wait_recv()
    surface = sst_in[0] + sst_in[1]
    col = iota((8, LANES), 1)
    surface = jnp.where(col // NY == iota((8, LANES), 0), surface, 0.0)
    pick = jnp.where(lax.rem(iota((COLS, NY), 0), NY) == iota((COLS, NY), 1), F32(1), F32(0))
    sst_ref[...] = jnp.dot(surface, pick, precision=HIGH, preferred_element_type=F32)

    stores.append(store(4, sst_ref, sst_hbm))
    pltpu.make_async_copy(mid, came, go_send).wait()
    pltpu.make_async_copy(back, mid2, back_send).wait()
    for c in sends:
        c.wait_send()
    for c in sst_copies:
        c.wait_send()
    for c in stores:
        c.wait()


def hand_over(*refs):
    src, dst, held, sems = refs[:5], refs[5:10], refs[10:15], refs[15]
    loads = [pltpu.make_async_copy(src[i], held[i], sems.at[0, i]) for i in range(5)]
    stores = [pltpu.make_async_copy(held[i], dst[i], sems.at[1, i]) for i in range(5)]
    for c in loads:
        c.start()
    for a, b in zip(loads, stores):
        a.wait()
        b.start()
    for c in stores:
        c.wait()


def on_device(
    state, u_wind, v_wind, mixing, stretch_order, remap_index, remap_weight, land_sea, ocean_temp, ocean_mixing,
):
    hbm = pl.BlockSpec(memory_space=pltpu.HBM)
    dma = pltpu.SemaphoreType.DMA
    big = pltpu.VMEM((COLS, CH), F32)
    split = pltpu.VMEM((4, 32, CH), F32)
    scratch = [
        pltpu.VMEM((CH, CH), BF16), pltpu.VMEM((CH, CH), BF16),
        pltpu.VMEM((COLS, LANES), F32), pltpu.VMEM((COLS, LANES), F32),
        big, big, big,
        pltpu.VMEM((NX, CH), F32), pltpu.VMEM((NX, CH), F32),
        pltpu.VMEM((2, NY, CH), F32), pltpu.VMEM((2, NY, CH), F32),
        pltpu.VMEM((2, NX, CH), F32),
        pltpu.VMEM((2, 1, CH), F32), pltpu.VMEM((2, 1, CH), F32),
        big, split,
        pltpu.VMEM((2, COLS, LANES), F32),
        pltpu.VMEM((8, LANES), F32), pltpu.VMEM((8, LANES), F32),
        pltpu.VMEM((8, LANES), F32), pltpu.VMEM((2, 8, LANES), F32),
        split, big, big,
        pltpu.VMEM((2, 2, 1, CH), F32),
        dma((2, 5)), dma((2, 5)), dma, dma, dma, dma, dma((2,)), dma((2,)),
        dma, dma, dma, dma((4,)),
        split, split, pltpu.SemaphoreType.REGULAR,
        dma((4, 3)), dma((4, 3)), dma, dma((4, 3)), dma((4, 3)), dma((4,)),
    ]
    out_shape = [
            jax.ShapeDtypeStruct((COLS, CH), F32),
            jax.ShapeDtypeStruct((64, LEV), F32),
            jax.ShapeDtypeStruct((64, LEV * NF), F32),
            jax.ShapeDtypeStruct(ocean_temp.shape, F32),
            jax.ShapeDtypeStruct((NX, NY), F32),
    ]
    ins = (
        state.reshape(COLS, CH),
        u_wind.reshape(COLS, HL),
        v_wind.reshape(COLS, HL),
        mixing,
        stretch_order.reshape(1, COLS),
        remap_index.T,
        remap_weight.T,
        land_sea.reshape(1, COLS),
        ocean_temp,
        ocean_mixing,
    )
    held = [pltpu.VMEM(a.shape, a.dtype) for a in (*ins, *out_shape)]
    outs = pl.pallas_call(
        window_kernel,
        out_shape=out_shape,
        in_specs=[hbm] * 10,
        out_specs=[hbm] * 5,
        scratch_shapes=[*held, dma((10,)), dma((5,)), *scratch],
        compiler_params=pltpu.CompilerParams(
            collective_id=0, has_side_effects=True, vmem_limit_bytes=56 * 2**20
        ),
        name="window",
    )(*ins)
    outs = pl.pallas_call(
        hand_over,
        out_shape=out_shape,
        in_specs=[hbm] * 5,
        out_specs=[hbm] * 5,
        scratch_shapes=[*(pltpu.VMEM(a.shape, a.dtype) for a in out_shape), dma((2, 5))],
        compiler_params=pltpu.CompilerParams(vmem_limit_bytes=56 * 2**20),
        name="outputs",
    )(*outs)
    return (outs[0].reshape(state.shape), *outs[1:])


def solution(mesh):
    placed = (
        P("blk", "sec", "lev"),
        P("blk", "sec", "lev"),
        P("blk", "sec", "lev"),
        P(),
        P(("sec", "blk")),
        P(("sec", "blk", "lev"), None),
        P(("sec", "blk", "lev"), None),
        P(("sec", "blk", "lev")),
        P(None, ("sec", "blk", "lev")),
        P(),
    )
    return jax.shard_map(
        on_device,
        mesh=mesh,
        in_specs=placed,
        out_specs=(
            P("blk", "sec", "lev"),
            P(("sec", "blk", "lev"), None),
            P(("sec", "blk", "lev"), None),
            P(None, ("sec", "blk", "lev")),
            P("blk", "sec"),
        ),
        check_vma=False,
    )
```

```python
import functools
import math

import jax
import jax.numpy as jnp
import numpy as np
from jax import lax
from jax.experimental import pallas as pl
from jax.experimental.pallas import tpu as pltpu
from jax.sharding import PartitionSpec as P

NP = 4
LEV = 128
NF = 12
NX, NY = 8, 16
COLS = NX * NY
HL = 64
CH = HL * NF
NBLK = 128
LANES = 128
NQ = CH // LANES
F32 = jnp.float32
BF16 = jnp.bfloat16
HIGH = lax.Precision.HIGHEST
MESH = pl.DeviceIdType.MESH


def gll_derivative():
    nodes = np.array([-1.0, -1.0 / math.sqrt(5.0), 1.0 / math.sqrt(5.0), 1.0])
    count = nodes.shape[0]
    bary = np.ones(count)
    for j in range(count):
        for k in range(count):
            if k != j:
                bary[j] = bary[j] / (nodes[j] - nodes[k])
    table = np.zeros((count, count))
    for i in range(count):
        for j in range(count):
            if i != j:
                table[i, j] = bary[j] / bary[i] / (nodes[i] - nodes[j])
        table[i, i] = -np.sum(table[i])
    return table.astype(np.float32)


def iota(shape, dim):
    return lax.broadcasted_iota(jnp.int32, shape, dim)


def split2(x):
    hi = x.astype(BF16)
    lo = (x - hi.astype(F32)).astype(BF16)
    return hi, lo


def dot(a, b):
    return jnp.dot(a, b, preferred_element_type=F32)


def dot3(a, b_hi, b_lo):
    hi, lo = split2(a)
    return dot(hi, b_hi) + dot(lo, b_hi) + dot(hi, b_lo)


def remote(src, dst, send, recv, device):
    return pltpu.make_async_remote_copy(
        src_ref=src, dst_ref=dst, send_sem=send, recv_sem=recv,
        device_id=device, device_id_type=MESH,
    )


def row(ref, r):
    return ref.at[pl.ds(r, 1)]


def advect(field_ref, uw_ref, vw_ref, out_ref, table, part):
    y8 = iota((8, LANES), 0)
    at = lax.rem(y8, NP)
    coefs = {}
    for d in range(-3, 4):
        c = jnp.zeros((8, LANES), F32)
        for i in range(NP):
            if 0 <= i + d < NP:
                c = jnp.where(at == i, F32(table[i, i + d]), c)
        coefs[d] = c[None]
    for q in range(part * 3, part * 3 + 3):
        lanes = slice(q * LANES, (q + 1) * LANES)
        for e in range(2):
            rows = slice(e * 64, (e + 1) * 64)
            f = field_ref[rows, lanes].reshape(NP, NY, LANES)
            dx = []
            for i in range(NP):
                acc = F32(table[i, 0]) * f[0]
                for j in range(1, NP):
                    acc = acc + F32(table[i, j]) * f[j]
                dx.append(acc[None])
            dx = jnp.concatenate(dx, axis=0).reshape(64, LANES)
            f8 = f.reshape(8, 8, LANES)
            dy = coefs[0] * f8
            for d in (-3, -2, -1, 1, 2, 3):
                dy = dy + coefs[d] * pltpu.roll(f8, (-d) % 8, axis=1)
            dy = dy.reshape(64, LANES)
            out_ref[rows, lanes] = f.reshape(64, LANES) - (
                uw_ref[rows, :] * dx + vw_ref[rows, :] * dy
            )


def average(a_ref, x_from_left, x_from_right, edge_ref, cor_l, cor_r, out_ref, s, part):
    y = iota((NY, LANES), 0)
    i = lax.rem(y, NP)
    at_edge = ((y == NY - 1) & (s == 0)) | ((y == 0) & (s == 1))
    closed = ((y == NY - 1) & (s == 1)) | ((y == 0) & (s == 0))
    inside = ((i == 0) | (i == NP - 1)) & jnp.logical_not(closed)
    for q in range(part * 3, part * 3 + 3):
        lanes = slice(q * LANES, (q + 1) * LANES)
        a = [a_ref[x * NY:(x + 1) * NY, lanes] for x in range(NX)]
        e = edge_ref[:, lanes]
        e = [e[x:x + 1] for x in range(NX)]
        a[0] = 0.5 * (a[0] + x_from_left[:, lanes])
        a[7] = 0.5 * (a[7] + x_from_right[:, lanes])
        a[3] = a[4] = 0.5 * (a[3] + a[4])
        e[0] = 0.5 * (e[0] + cor_l[0:1, lanes])
        e[7] = 0.5 * (e[7] + cor_r[0:1, lanes])
        e[3] = e[4] = 0.5 * (e[3] + e[4])
        for x in range(NX):
            f = a[x]
            up = pltpu.roll(f, NY - 1, axis=0)
            dn = pltpu.roll(f, 1, axis=0)
            nb = jnp.where(i == NP - 1, up, dn)
            nb = jnp.where(at_edge, jnp.broadcast_to(e[x], (NY, LANES)), nb)
            out_ref[x * NY:(x + 1) * NY, lanes] = jnp.where(inside, 0.5 * (f + nb), f)


def window_kernel(
    state_hbm, u_hbm, v_hbm, mixing_hbm, order_hbm, index_hbm, weight_hbm, sea_hbm, temp_hbm, omix_hbm,
    adv_hbm, rate_hbm, rows_hbm, curves_hbm, sst_hbm,
    state_ref, u_ref, v_ref, mixing_ref, order_ref, index_ref, weight_ref, sea_ref, temp_ref, omix_ref,
    adv_ref, rate_ref, rows_ref, curves_ref, sst_ref, in_sems, out_sems,
    perm, perm_t, uw, vw, field, adv1, adv2, edge1, edge2, xl, xr, ye, cl, cr,
    gone, came, tv, flux_out, flux_in, sst_out, sst_in, back, home, mixed, spare,
    halo_send, halo_recv, tv_send, tv_recv, flux_send, flux_recv, sst_send, sst_recv,
    go_send, go_recv, back_send, back_recv,
    mid, mid2, plane, mid_send, mid_recv, stay_sem, home_send, home_recv, home_stay,
):
    s, b, l = lax.axis_index("sec"), lax.axis_index("blk"), lax.axis_index("lev")
    table = gll_derivative()
    left, right = lax.rem(b + NBLK - 1, NBLK), lax.rem(b + 1, NBLK)

    loads = [
        pltpu.make_async_copy(src, dst, in_sems.at[i])
        for i, (src, dst) in enumerate((
            (state_hbm, state_ref), (u_hbm, u_ref), (v_hbm, v_ref), (order_hbm, order_ref), (mixing_hbm, mixing_ref),
            (index_hbm, index_ref), (weight_hbm, weight_ref), (sea_hbm, sea_ref), (temp_hbm, temp_ref), (omix_hbm, omix_ref),
        ))
    ]
    for c in loads:
        c.start()

    barrier = pltpu.get_barrier_semaphore()

    def greet(device):
        pl.semaphore_signal(barrier, inc=1, device_id=device, device_id_type=MESH)

    bx, by, bz = b // 32, lax.rem(b // 4, 8), lax.rem(b, 4)
    pair = by // 2
    along_x = [(s, lax.rem(bx + d, 4) * 32 + lax.rem(b, 32), l) for d in range(1, 4)]
    along_y = [(s, bx * 32 + lax.rem(by + d, 8) * 4 + bz, l) for d in range(1, 8)]
    along_z = [(s, bx * 32 + by * 4 + lax.rem(bz + d, 4), l) for d in range(1, 4)]
    along_z += [(s, bx * 32 + by * 4 + lax.rem(bz + d, 4), 1 - l) for d in range(4)]
    near = [(s, left, l), (s, right, l), (1 - s, b, l), (1 - s, left, l), (1 - s, right, l), (1 - s, b, 1 - l)]
    near += along_x + along_z + along_y
    for device in near:
        greet(device)

    for q in range(NQ):
        wide = (CH, LANES)
        to = iota(wide, 1) + q * LANES
        perm[:, q * LANES:(q + 1) * LANES] = jnp.where(
            iota(wide, 0) == lax.rem(to, HL) * NF + to // HL, F32(1), F32(0)
        ).astype(BF16)
        perm_t[:, q * LANES:(q + 1) * LANES] = jnp.where(
            to == lax.rem(iota(wide, 0), HL) * NF + iota(wide, 0) // HL, F32(1), F32(0)
        ).astype(BF16)
    for c in loads[:3]:
        c.wait()
    hi, lo = split2(state_ref[...])
    field[...] = dot(hi, perm[...]) + dot(lo, perm[...])
    for ref, wind in ((uw, u_ref), (vw, v_ref)):
        w = F32(0.1) * wind[...]
        ref[...] = jnp.concatenate([w, w], axis=1)

    for c in loads[3:]:
        c.wait()

    square = (COLS, COLS)
    hot_t = jnp.where(iota(square, 0) == order_ref[...], F32(1), F32(0))
    hot = hot_t.T.astype(BF16)
    hot_t = hot_t.astype(BF16)

    mt = mixing_ref[...].T
    lane = iota((HL, LANES), 1)
    blocks = []
    for li in range(2):
        part = mt[li * HL:(li + 1) * HL]
        turned = pltpu.roll(part, HL, axis=1)
        zero = jnp.zeros_like(part)
        blocks.append(jnp.concatenate([jnp.where(lane < HL, part, zero), jnp.where(lane < HL, turned, zero)], axis=1))
        blocks.append(jnp.concatenate([jnp.where(lane < HL, zero, turned), jnp.where(lane < HL, zero, part)], axis=1))
    pair_hi, pair_lo = split2(jnp.concatenate(blocks, axis=0))

    sea = sea_ref[...].astype(F32)
    weigh = jnp.zeros(square, F32)
    for m in range(4):
        weigh = weigh + jnp.where(iota(square, 0) == index_ref[m:m + 1, :], weight_ref[m:m + 1, :], F32(0))
    calm = jnp.dot(omix_ref[...], temp_ref[...], precision=HIGH, preferred_element_type=F32)

    sends = []

    def exchange(turn, part):
        a, edge = ((adv1, edge1), (adv2, edge2))[turn]
        lanes = slice(part * CH // 2, (part + 1) * CH // 2)
        cut = pl.ds(part * CH // 2, CH // 2)
        for x in range(NX):
            bottom, top = a[x * NY:x * NY + 1, lanes], a[(x + 1) * NY - 1:(x + 1) * NY, lanes]
            edge[x:x + 1, lanes] = jnp.where(s == 0, top, bottom)
        parts = (
            (a.at[pl.ds(0, NY), cut], xr.at[turn, :, cut], (s, left, l)),
            (a.at[pl.ds(COLS - NY, NY), cut], xl.at[turn, :, cut], (s, right, l)),
            (edge.at[:, cut], ye.at[turn, :, cut], (1 - s, b, l)),
            (edge.at[pl.ds(0, 1), cut], cr.at[turn, :, cut], (1 - s, left, l)),
            (edge.at[pl.ds(NX - 1, 1), cut], cl.at[turn, :, cut], (1 - s, right, l)),
        )
        copies = [
            remote(src, dst, halo_send.at[turn, part, i], halo_recv.at[turn, part, i], device)
            for i, (src, dst, device) in enumerate(parts)
        ]
        for c in copies:
            c.start()
        sends.extend(copies)
        return copies

    def settle(turn, part, copies):
        for c in copies:
            c.wait_recv()
        a = (adv1, adv2)[turn]
        average(a, xl.at[turn], xr.at[turn], ye.at[turn], cl.at[turn], cr.at[turn], field, s, part)

    for part in range(2):
        advect(field, uw, vw, adv1, table, part)
    pl.semaphore_wait(barrier, len(near))
    first = [exchange(0, part) for part in range(2)]
    for device in along_y:
        pl.semaphore_signal(plane, inc=1, device_id=device, device_id_type=MESH)
    second = []
    for part in range(2):
        settle(0, part, first[part])
        advect(field, uw, vw, adv2, table, part)
        second.append(exchange(1, part))

    lane128 = iota((COLS, LANES), 1)
    here = by * 4 + bz

    def rows_of(turned):
        return pl.ds(pl.multiple_of(turned * 8, 8), 8)

    def block(x, turned):
        return pl.ds(pl.multiple_of(x * 32 + turned * 8, 8), 8)

    def in_pair(c, j):
        y = lax.rem(pair + c, 4) * 2 + lax.rem(by + j // 8, 2)
        return y * 4 + lax.rem(bz + j // 2, 4), lax.rem(l + j, 2)

    across = []
    for part in range(2):
        settle(1, part, second[part])
        if part == 0:
            tv[pl.ds(l, 1)] = jnp.where(
                lane128 < HL, field[:, 0:LANES], pltpu.roll(field[:, LANES:2 * LANES], HL, axis=1)
            )[None]
            tv_copy = remote(tv.at[l], tv.at[l], tv_send, tv_recv, (s, b, 1 - l))
            tv_copy.start()
            sends.append(tv_copy)
        lanes = slice(part * CH // 2, (part + 1) * CH // 2)
        cut = pl.ds(part * CH // 2, CH // 2)
        hi, lo = split2(field[:, lanes])
        gone[:, lanes] = dot(hot, hi) + dot(hot, lo)
        for c in range(4):
            turned = lax.rem(pair + c, 4)
            for d in range(3):
                copy = remote(
                    gone.at[block(lax.rem(bx + d + 1, 4), turned), cut], mid.at[bx, rows_of(turned), cut],
                    mid_send.at[c, d, part], mid_recv.at[c, d, part], along_x[d],
                )
                copy.start()
                across.append((c, copy))
                sends.append(copy)
    stay = pltpu.make_async_copy(gone.at[pl.ds(pl.multiple_of(bx * 32, 32), 32)], mid.at[bx], stay_sem)
    stay.start()

    pl.semaphore_wait(plane, len(along_y))
    stay.wait()

    def both_x(ref, h, place):
        return ref.at[pl.ds(h * 2, 2), pl.ds(place, 1)]

    for c in range(4):
        for k, copy in across:
            if k == c:
                copy.wait_recv()

        def send_columns(j, carry, c=c):
            place, h = in_pair(c, j)
            remote(
                both_x(mid, h, place), both_x(came, l, here), go_send, go_recv.at[c], (s, bx * 32 + place, h)
            ).start()
            return carry

        lax.fori_loop(1 if c == 0 else 0, 16, send_columns, 0, unroll=True)
        if c == 0:
            pltpu.make_async_copy(both_x(mid, l, here), both_x(came, l, here), go_recv.at[0]).start()
            pltpu.make_async_copy(both_x(mid, l, here), spare.at[0], go_send).start()

    lane64 = iota((64, LANES), 1)
    for step in range(2):
        turns = []
        for c in (step * 2, step * 2 + 1):
            turns.append(lax.rem(pair + 4 - c, 4))
            arrived = came.at[:, rows_of(turns[-1])]
            pltpu.make_async_copy(arrived, arrived, go_recv.at[c]).wait()
        loaded = [came[:, rows_of(t), :] for t in turns]
        wide = jnp.concatenate(
            [
                jnp.concatenate(
                    [
                        jnp.concatenate(
                            [a[h * 2:h * 2 + 2, :, q * LANES:(q + 1) * LANES].reshape(16, LANES) for a in loaded], axis=0
                        )
                        for h in range(2)
                    ],
                    axis=1,
                )
                for q in range(NQ)
            ],
            axis=0,
        )
        done = dot3(wide, pair_hi, pair_lo)
        for q in range(NQ):
            for h in range(2):
                mixed[h * 32:(h + 1) * 32, q * LANES:(q + 1) * LANES] = done[
                    q * 32:(q + 1) * 32, h * LANES:(h + 1) * LANES
                ]
        temper = mixed[:, 0:LANES]
        vapour = mixed[:, LANES:2 * LANES]
        condense = jnp.maximum(vapour - 0.5 * jnp.exp(0.3 * temper), 0.0)
        mixed[:, 0:LANES] = jnp.where(lane64 < HL, temper + 0.5 * condense, temper)
        mixed[:, LANES:2 * LANES] = jnp.where(lane64 < HL, vapour - condense, vapour)
        hi, lo = split2(mixed[...])
        ready = dot(hi, perm_t[...]) + dot(lo, perm_t[...])
        for n, t in enumerate(turns):
            for h in range(2):
                for x in range(2):
                    at = h * 32 + n * 16 + x * 8
                    back[h * 2 + x, rows_of(t), :] = ready[at:at + 8]
        rate = jnp.where(lane64[0:32] < HL, condense[0:32], pltpu.roll(condense[32:64], HL, axis=1))
        for n, t in enumerate(turns):
            for x in range(2):
                rate_ref[block(x, t), :] = rate[n * 16 + x * 8:n * 16 + x * 8 + 8]
        for c in (step * 2, step * 2 + 1):

            def send_rows(j, carry, c=c):
                place, k = in_pair((4 - c) % 4, j)
                remote(
                    both_x(back, k, place), both_x(mid2, l, here), back_send, back_recv.at[c], (s, bx * 32 + place, k)
                ).start()
                return carry

            lax.fori_loop(1 if c == 0 else 0, 16, send_rows, 0, unroll=True)
            if c == 0:
                pltpu.make_async_copy(both_x(back, l, here), both_x(mid2, l, here), back_recv.at[0]).start()
                pltpu.make_async_copy(both_x(back, l, here), spare.at[1], back_send).start()

    tv_copy.wait_recv()
    whole = jnp.concatenate([tv[0], tv[1]], axis=1)
    both = dot3(whole, pair_hi, pair_lo)
    level = lax.rem(lane128, HL)
    total = jnp.zeros((COLS, LANES), F32)
    for lo_ in range(2):
        part = both[:, lo_ * LANES:(lo_ + 1) * LANES]
        vapour = pltpu.roll(part, HL, axis=1)
        condense = jnp.maximum(vapour - 0.5 * jnp.exp(0.3 * part), 0.0)
        heat = part + 0.5 * condense
        moist = vapour - condense
        w = (1.0 + (level + lo_ * HL).astype(F32) / LEV) / math.sqrt(LEV)
        total = total + jnp.where(lane128 < HL, w * (0.5 * heat + 0.5 * moist), 0.0)
    flux = jnp.sum(total.T, axis=0, keepdims=True)
    flux_out[...] = jnp.broadcast_to(flux, (8, LANES))
    flux_copy = remote(flux_out, flux_in, flux_send, flux_recv, (1 - s, b, l))
    flux_copy.start()
    sends.append(flux_copy)

    def pass_rows(c):
        turned = lax.rem(pair + c, 4)
        arrived = mid2.at[:, rows_of(turned)]
        pltpu.make_async_copy(arrived, arrived, back_recv.at[c]).wait()
        for d in range(3):
            copy = remote(
                mid2.at[lax.rem(bx + d + 1, 4), rows_of(turned)], home.at[block(bx, turned)],
                home_send.at[c, d], home_recv.at[c, d], along_x[d],
            )
            copy.start()
            last.append(copy)
        copy = pltpu.make_async_copy(mid2.at[bx, rows_of(turned)], home.at[block(bx, turned)], home_stay.at[c])
        copy.start()
        stays.append(copy)

    last, stays = [], []
    pass_rows(0)
    pass_rows(1)

    flux_copy.wait_recv()
    forcing = jnp.dot(flux_in[...], weigh, precision=HIGH, preferred_element_type=F32)
    forcing = sea * forcing[0:1]
    curves = calm + omix_ref[:, 0:1] * forcing
    curves_ref[...] = curves
    entry = jnp.broadcast_to(sea * curves[0:1], (8, LANES))
    sst_out[...] = lax.dot_general(
        entry, weigh, (((1,), (1,)), ((), ())), precision=HIGH, preferred_element_type=F32
    )
    sst_copies = [
        remote(sst_out, sst_in.at[l], sst_send.at[k], sst_recv.at[l], (1 - s, b, k)) for k in range(2)
    ]
    for c in sst_copies:
        c.start()

    pass_rows(2)
    pass_rows(3)
    for h in range(2):
        rows_ref[:, h * CH:(h + 1) * CH] = back[h * 2:h * 2 + 2].reshape(64, CH)

    def store(i, src, dst):
        c = pltpu.make_async_copy(src, dst, out_sems.at[i])
        c.start()
        return c

    stores = [store(0, rate_ref, rate_hbm), store(1, rows_ref, rows_hbm), store(2, curves_ref, curves_hbm)]

    for k in range(2):
        remote(sst_out, sst_in.at[k], sst_send.at[k], sst_recv.at[k], (1 - s, b, k)).wait_recv()
    surface = sst_in[0] + sst_in[1]
    col = iota((8, LANES), 1)
    surface = jnp.where(col // NY == iota((8, LANES), 0), surface, 0.0)
    pick = jnp.where(lax.rem(iota((COLS, NY), 0), NY) == iota((COLS, NY), 1), F32(1), F32(0))
    sst_ref[...] = jnp.dot(surface, pick, precision=HIGH, preferred_element_type=F32)

    stores.append(store(4, sst_ref, sst_hbm))

    for c in stays:
        c.wait()
    for c in last:
        c.wait_recv()
    sends += last
    hi, lo = split2(home[...])
    adv_ref[...] = dot(hot_t, hi) + dot(hot_t, lo)

    stores.append(store(3, adv_ref, adv_hbm))

    pltpu.make_async_copy(mid, came, go_send).wait()
    pltpu.make_async_copy(back, mid2, back_send).wait()
    for c in sends:
        c.wait_send()
    for c in sst_copies:
        c.wait_send()
    for c in stores:
        c.wait()


def hand_over(*refs):
    src, dst, held, sems = refs[:5], refs[5:10], refs[10:15], refs[15]
    loads = [pltpu.make_async_copy(src[i], held[i], sems.at[0, i]) for i in range(5)]
    stores = [pltpu.make_async_copy(held[i], dst[i], sems.at[1, i]) for i in range(5)]
    for c in loads:
        c.start()
    for a, b in zip(loads, stores):
        a.wait()
        b.start()
    for c in stores:
        c.wait()


def on_device(
    state, u_wind, v_wind, mixing, stretch_order, remap_index, remap_weight, land_sea, ocean_temp, ocean_mixing,
):
    hbm = pl.BlockSpec(memory_space=pltpu.HBM)
    dma = pltpu.SemaphoreType.DMA
    big = pltpu.VMEM((COLS, CH), F32)
    split = pltpu.VMEM((4, 32, CH), F32)
    scratch = [
        pltpu.VMEM((CH, CH), BF16), pltpu.VMEM((CH, CH), BF16),
        pltpu.VMEM((COLS, LANES), F32), pltpu.VMEM((COLS, LANES), F32),
        big, big, big,
        pltpu.VMEM((NX, CH), F32), pltpu.VMEM((NX, CH), F32),
        pltpu.VMEM((2, NY, CH), F32), pltpu.VMEM((2, NY, CH), F32),
        pltpu.VMEM((2, NX, CH), F32),
        pltpu.VMEM((2, 1, CH), F32), pltpu.VMEM((2, 1, CH), F32),
        big, split,
        pltpu.VMEM((2, COLS, LANES), F32),
        pltpu.VMEM((8, LANES), F32), pltpu.VMEM((8, LANES), F32),
        pltpu.VMEM((8, LANES), F32), pltpu.VMEM((2, 8, LANES), F32),
        split, big, pltpu.VMEM((64, CH), F32),
        pltpu.VMEM((2, 2, 1, CH), F32),
        dma((2, 2, 5)), dma((2, 2, 5)), dma, dma, dma, dma, dma((2,)), dma((2,)),
        dma, dma((4,)), dma, dma((4,)),
        split, split, pltpu.SemaphoreType.REGULAR,
        dma((4, 3, 2)), dma((4, 3, 2)), dma, dma((4, 3)), dma((4, 3)), dma((4,)),
    ]
    out_shape = [
            jax.ShapeDtypeStruct((COLS, CH), F32),
            jax.ShapeDtypeStruct((64, LEV), F32),
            jax.ShapeDtypeStruct((64, LEV * NF), F32),
            jax.ShapeDtypeStruct(ocean_temp.shape, F32),
            jax.ShapeDtypeStruct((NX, NY), F32),
    ]
    ins = (
        state.reshape(COLS, CH),
        u_wind.reshape(COLS, HL),
        v_wind.reshape(COLS, HL),
        mixing,
        stretch_order.reshape(1, COLS),
        remap_index.T,
        remap_weight.T,
        land_sea.reshape(1, COLS),
        ocean_temp,
        ocean_mixing,
    )
    held = [pltpu.VMEM(a.shape, a.dtype) for a in (*ins, *out_shape)]
    outs = pl.pallas_call(
        window_kernel,
        out_shape=out_shape,
        in_specs=[hbm] * 10,
        out_specs=[hbm] * 5,
        scratch_shapes=[*held, dma((10,)), dma((5,)), *scratch],
        compiler_params=pltpu.CompilerParams(
            collective_id=0, has_side_effects=True, vmem_limit_bytes=56 * 2**20
        ),
        name="window",
    )(*ins)
    outs = pl.pallas_call(
        hand_over,
        out_shape=out_shape,
        in_specs=[hbm] * 5,
        out_specs=[hbm] * 5,
        scratch_shapes=[*(pltpu.VMEM(a.shape, a.dtype) for a in out_shape), dma((2, 5))],
        compiler_params=pltpu.CompilerParams(vmem_limit_bytes=56 * 2**20),
        name="outputs",
    )(*outs)
    return (outs[0].reshape(state.shape), *outs[1:])


def solution(mesh):
    placed = (
        P("blk", "sec", "lev"),
        P("blk", "sec", "lev"),
        P("blk", "sec", "lev"),
        P(),
        P(("sec", "blk")),
        P(("sec", "blk", "lev"), None),
        P(("sec", "blk", "lev"), None),
        P(("sec", "blk", "lev")),
        P(None, ("sec", "blk", "lev")),
        P(),
    )
    return jax.shard_map(
        on_device,
        mesh=mesh,
        in_specs=placed,
        out_specs=(
            P("blk", "sec", "lev"),
            P(("sec", "blk", "lev"), None),
            P(("sec", "blk", "lev"), None),
            P(None, ("sec", "blk", "lev")),
            P("blk", "sec"),
        ),
        check_vma=False,
    )
```

```python
import functools
import math

import jax
import jax.numpy as jnp
import numpy as np
from jax import lax
from jax.experimental import pallas as pl
from jax.experimental.pallas import tpu as pltpu
from jax.sharding import PartitionSpec as P

NP = 4
LEV = 128
NF = 12
NX, NY = 8, 16
COLS = NX * NY
HL = 64
CH = HL * NF
NBLK = 128
LANES = 128
NQ = CH // LANES
PAIRS = (2, 0, 1, 3)
F32 = jnp.float32
BF16 = jnp.bfloat16
HIGH = lax.Precision.HIGHEST
MESH = pl.DeviceIdType.MESH


def gll_derivative():
    nodes = np.array([-1.0, -1.0 / math.sqrt(5.0), 1.0 / math.sqrt(5.0), 1.0])
    count = nodes.shape[0]
    bary = np.ones(count)
    for j in range(count):
        for k in range(count):
            if k != j:
                bary[j] = bary[j] / (nodes[j] - nodes[k])
    table = np.zeros((count, count))
    for i in range(count):
        for j in range(count):
            if i != j:
                table[i, j] = bary[j] / bary[i] / (nodes[i] - nodes[j])
        table[i, i] = -np.sum(table[i])
    return table.astype(np.float32)


def iota(shape, dim):
    return lax.broadcasted_iota(jnp.int32, shape, dim)


def split2(x):
    hi = x.astype(BF16)
    lo = (x - hi.astype(F32)).astype(BF16)
    return hi, lo


def dot(a, b):
    return jnp.dot(a, b, preferred_element_type=F32)


def dot3(a, b_hi, b_lo):
    hi, lo = split2(a)
    both = dot(jnp.concatenate([hi, lo], axis=0), b_hi)
    return both[:a.shape[0]] + both[a.shape[0]:] + dot(hi, b_lo)


def dot_rows(a, hot):
    both = dot(jnp.concatenate(split2(a), axis=0), hot)
    return both[:a.shape[0]] + both[a.shape[0]:]


def pick_rows(hot, a):
    return dot(jnp.concatenate([hot, hot], axis=1), jnp.concatenate(split2(a), axis=0))


def remote(src, dst, send, recv, device):
    return pltpu.make_async_remote_copy(
        src_ref=src, dst_ref=dst, send_sem=send, recv_sem=recv,
        device_id=device, device_id_type=MESH,
    )


def row(ref, r):
    return ref.at[pl.ds(r, 1)]


def advect(field_ref, uw_ref, vw_ref, out_ref, table, part):
    y8 = iota((8, LANES), 0)
    at = lax.rem(y8, NP)
    coefs = {}
    for d in range(-3, 4):
        c = jnp.zeros((8, LANES), F32)
        for i in range(NP):
            if 0 <= i + d < NP:
                c = jnp.where(at == i, F32(table[i, i + d]), c)
        coefs[d] = c[None]
    for q in range(part * 3, part * 3 + 3):
        lanes = slice(q * LANES, (q + 1) * LANES)
        for e in range(2):
            rows = slice(e * 64, (e + 1) * 64)
            f = field_ref[rows, lanes].reshape(NP, NY, LANES)
            dx = []
            for i in range(NP):
                acc = F32(table[i, 0]) * f[0]
                for j in range(1, NP):
                    acc = acc + F32(table[i, j]) * f[j]
                dx.append(acc[None])
            dx = jnp.concatenate(dx, axis=0).reshape(64, LANES)
            f8 = f.reshape(8, 8, LANES)
            dy = coefs[0] * f8
            for d in (-3, -2, -1, 1, 2, 3):
                dy = dy + coefs[d] * pltpu.roll(f8, (-d) % 8, axis=1)
            dy = dy.reshape(64, LANES)
            out_ref[rows, lanes] = f.reshape(64, LANES) - (
                uw_ref[rows, :] * dx + vw_ref[rows, :] * dy
            )


def average(a_ref, x_from_left, x_from_right, edge_ref, cor_l, cor_r, out_ref, s, part):
    y = iota((NY, LANES), 0)
    i = lax.rem(y, NP)
    at_edge = ((y == NY - 1) & (s == 0)) | ((y == 0) & (s == 1))
    closed = ((y == NY - 1) & (s == 1)) | ((y == 0) & (s == 0))
    inside = ((i == 0) | (i == NP - 1)) & jnp.logical_not(closed)
    for q in range(part * 3, part * 3 + 3):
        lanes = slice(q * LANES, (q + 1) * LANES)
        a = [a_ref[x * NY:(x + 1) * NY, lanes] for x in range(NX)]
        e = edge_ref[:, lanes]
        e = [e[x:x + 1] for x in range(NX)]
        a[0] = 0.5 * (a[0] + x_from_left[:, lanes])
        a[7] = 0.5 * (a[7] + x_from_right[:, lanes])
        a[3] = a[4] = 0.5 * (a[3] + a[4])
        e[0] = 0.5 * (e[0] + cor_l[0:1, lanes])
        e[7] = 0.5 * (e[7] + cor_r[0:1, lanes])
        e[3] = e[4] = 0.5 * (e[3] + e[4])
        for x in range(NX):
            f = a[x]
            up = pltpu.roll(f, NY - 1, axis=0)
            dn = pltpu.roll(f, 1, axis=0)
            nb = jnp.where(i == NP - 1, up, dn)
            nb = jnp.where(at_edge, jnp.broadcast_to(e[x], (NY, LANES)), nb)
            out_ref[x * NY:(x + 1) * NY, lanes] = jnp.where(inside, 0.5 * (f + nb), f)


def window_kernel(
    state_hbm, u_hbm, v_hbm, mixing_hbm, order_hbm, index_hbm, weight_hbm, sea_hbm, temp_hbm, omix_hbm,
    home, rate_hbm, rows_hbm, curves_hbm, sst_hbm,
    state_ref, u_ref, v_ref, mixing_ref, order_ref, index_ref, weight_ref, sea_ref, temp_ref, omix_ref,
    rate_ref, rows_ref, curves_ref, sst_ref, in_sems, out_sems,
    perm, perm_t, uw, vw, field, adv1, adv2, edge1, edge2, xl, xr, ye, cl, cr,
    gone, came, tv, flux_out, flux_in, sst_out, sst_in, back, mixed, spare,
    halo_send, halo_recv, tv_send, tv_recv, flux_send, flux_recv, sst_send, sst_recv,
    go_send, go_recv, back_send, back_recv,
    mid, mid2, plane, mid_send, mid_recv, stay_sem, home_send, home_recv, home_stay,
):
    s, b, l = lax.axis_index("sec"), lax.axis_index("blk"), lax.axis_index("lev")
    table = gll_derivative()
    left, right = lax.rem(b + NBLK - 1, NBLK), lax.rem(b + 1, NBLK)

    loads = [
        pltpu.make_async_copy(src, dst, in_sems.at[i])
        for i, (src, dst) in enumerate((
            (state_hbm, state_ref), (u_hbm, u_ref), (v_hbm, v_ref), (order_hbm, order_ref), (mixing_hbm, mixing_ref),
            (index_hbm, index_ref), (weight_hbm, weight_ref), (sea_hbm, sea_ref), (temp_hbm, temp_ref), (omix_hbm, omix_ref),
        ))
    ]
    for c in loads:
        c.start()

    barrier = pltpu.get_barrier_semaphore()

    def greet(device):
        pl.semaphore_signal(barrier, inc=1, device_id=device, device_id_type=MESH)

    bx, by, bz = b // 32, lax.rem(b // 4, 8), lax.rem(b, 4)
    pair = by // 2
    along_x = [(s, lax.rem(bx + d, 4) * 32 + lax.rem(b, 32), l) for d in range(1, 4)]
    along_y = [(s, bx * 32 + lax.rem(by + d, 8) * 4 + bz, l) for d in range(1, 8)]
    along_z = [(s, bx * 32 + by * 4 + lax.rem(bz + d, 4), l) for d in range(1, 4)]
    along_z += [(s, bx * 32 + by * 4 + lax.rem(bz + d, 4), 1 - l) for d in range(4)]
    near = [(s, left, l), (s, right, l), (1 - s, b, l), (1 - s, left, l), (1 - s, right, l), (1 - s, b, 1 - l)]
    near += along_x + along_z + along_y
    for device in near:
        greet(device)

    tall, wide = (CH, LANES), (1, LANES)
    for q in range(NQ):
        to = iota(wide, 1) + q * LANES
        perm[:, q * LANES:(q + 1) * LANES] = jnp.where(
            iota(tall, 0) == (to & (HL - 1)) * NF + (to >> 6), F32(1), F32(0)
        ).astype(BF16)
    for c in loads[:3]:
        c.wait()
    field[...] = dot_rows(state_ref[...], perm[...])
    for ref, wind in ((uw, u_ref), (vw, v_ref)):
        w = F32(0.1) * wind[...]
        ref[...] = jnp.concatenate([w, w], axis=1)


    sends = []

    def exchange(turn, part):
        a, edge = ((adv1, edge1), (adv2, edge2))[turn]
        lanes = slice(part * CH // 2, (part + 1) * CH // 2)
        cut = pl.ds(part * CH // 2, CH // 2)
        for x in range(NX):
            bottom, top = a[x * NY:x * NY + 1, lanes], a[(x + 1) * NY - 1:(x + 1) * NY, lanes]
            edge[x:x + 1, lanes] = jnp.where(s == 0, top, bottom)
        parts = (
            (a.at[pl.ds(0, NY), cut], xr.at[turn, :, cut], (s, left, l)),
            (a.at[pl.ds(COLS - NY, NY), cut], xl.at[turn, :, cut], (s, right, l)),
            (edge.at[:, cut], ye.at[turn, :, cut], (1 - s, b, l)),
            (edge.at[pl.ds(0, 1), cut], cr.at[turn, :, cut], (1 - s, left, l)),
            (edge.at[pl.ds(NX - 1, 1), cut], cl.at[turn, :, cut], (1 - s, right, l)),
        )
        copies = [
            remote(src, dst, halo_send.at[turn, part, i], halo_recv.at[turn, part, i], device)
            for i, (src, dst, device) in enumerate(parts)
        ]
        for c in copies:
            c.start()
        sends.extend(copies)
        return copies

    def settle(turn, part, copies):
        for c in copies:
            c.wait_recv()
        a = (adv1, adv2)[turn]
        average(a, xl.at[turn], xr.at[turn], ye.at[turn], cl.at[turn], cr.at[turn], field, s, part)

    for part in range(2):
        advect(field, uw, vw, adv1, table, part)
    pl.semaphore_wait(barrier, len(near))
    first = [exchange(0, part) for part in range(2)]
    for device in along_y:
        pl.semaphore_signal(plane, inc=1, device_id=device, device_id_type=MESH)
    source = iota(tall, 0)
    source = (source & (HL - 1)) * NF + (source >> 6)
    for q in range(NQ):
        perm_t[:, q * LANES:(q + 1) * LANES] = jnp.where(
            source == iota(wide, 1) + q * LANES, F32(1), F32(0)
        ).astype(BF16)
    for c in loads[3:]:
        c.wait()

    square = (COLS, COLS)
    hot_t = jnp.where(iota(square, 0) == order_ref[...], F32(1), F32(0))
    hot = hot_t.T.astype(BF16)

    mt = mixing_ref[...].T
    lane = iota((HL, LANES), 1)
    blocks = []
    for li in range(2):
        part = mt[li * HL:(li + 1) * HL]
        turned = pltpu.roll(part, HL, axis=1)
        zero = jnp.zeros_like(part)
        blocks.append(jnp.concatenate([jnp.where(lane < HL, part, zero), jnp.where(lane < HL, turned, zero)], axis=1))
        blocks.append(jnp.concatenate([jnp.where(lane < HL, zero, turned), jnp.where(lane < HL, zero, part)], axis=1))
    pair_hi, pair_lo = split2(jnp.concatenate(blocks, axis=0))

    sea = sea_ref[...].astype(F32)
    weigh = jnp.zeros(square, F32)
    for m in range(4):
        weigh = weigh + jnp.where(iota(square, 0) == index_ref[m:m + 1, :], weight_ref[m:m + 1, :], F32(0))
    calm = jnp.dot(omix_ref[...], temp_ref[...], precision=HIGH, preferred_element_type=F32)


    second = []
    for part in range(2):
        settle(0, part, first[part])
        advect(field, uw, vw, adv2, table, part)
        second.append(exchange(1, part))

    lane128 = iota((COLS, LANES), 1)
    here = by * 4 + bz

    def rows_of(turned):
        return pl.ds(pl.multiple_of(turned * 8, 8), 8)

    def block(x, turned):
        return pl.ds(pl.multiple_of(x * 32 + turned * 8, 8), 8)

    def in_pair(c, j):
        y = lax.rem(pair + c, 4) * 2 + lax.rem(by + j // 8, 2)
        return y * 4 + lax.rem(bz + j // 2, 4), lax.rem(l + j, 2)

    across = []
    for part in range(2):
        settle(1, part, second[part])
        if part == 0:
            tv[pl.ds(l, 1)] = jnp.where(
                lane128 < HL, field[:, 0:LANES], pltpu.roll(field[:, LANES:2 * LANES], HL, axis=1)
            )[None]
            tv_copy = remote(tv.at[l], tv.at[l], tv_send, tv_recv, (s, b, 1 - l))
            tv_copy.start()
            sends.append(tv_copy)
        lanes = slice(part * CH // 2, (part + 1) * CH // 2)
        cut = pl.ds(part * CH // 2, CH // 2)
        gone[:, lanes] = pick_rows(hot, field[:, lanes])
        for c in range(4):
            turned = lax.rem(pair + PAIRS[c], 4)
            for d in range(3):
                copy = remote(
                    gone.at[block(lax.rem(bx + d + 1, 4), turned), cut], mid.at[bx, rows_of(turned), cut],
                    mid_send.at[c, d, part], mid_recv.at[c, d, part], along_x[d],
                )
                copy.start()
                across.append((c, copy))
                sends.append(copy)
    stay = pltpu.make_async_copy(gone.at[pl.ds(pl.multiple_of(bx * 32, 32), 32)], mid.at[bx], stay_sem)
    stay.start()

    pl.semaphore_wait(plane, len(along_y))
    stay.wait()

    def both_x(ref, h, place):
        return ref.at[pl.ds(h * 2, 2), pl.ds(place, 1)]

    for c in range(4):
        for k, copy in across:
            if k == c:
                copy.wait_recv()

        def send_columns(j, carry, c=c):
            place, h = in_pair(PAIRS[c], j)
            remote(
                both_x(mid, h, place), both_x(came, l, here), go_send, go_recv.at[c], (s, bx * 32 + place, h)
            ).start()
            return carry

        lax.fori_loop(0 if PAIRS[c] else 1, 16, send_columns, 0, unroll=True)
        if PAIRS[c] == 0:
            pltpu.make_async_copy(both_x(mid, l, here), both_x(came, l, here), go_recv.at[c]).start()
            pltpu.make_async_copy(both_x(mid, l, here), spare.at[0], go_send).start()

    lane64 = iota((64, LANES), 1)
    for step in range(2):
        turns = []
        for c in (step * 2, step * 2 + 1):
            turns.append(lax.rem(pair + 4 - PAIRS[c], 4))
            arrived = came.at[:, rows_of(turns[-1])]
            pltpu.make_async_copy(arrived, arrived, go_recv.at[c]).wait()
        loaded = [came[:, rows_of(t), :] for t in turns]
        wide = jnp.concatenate(
            [
                jnp.concatenate(
                    [
                        jnp.concatenate(
                            [a[h * 2:h * 2 + 2, :, q * LANES:(q + 1) * LANES].reshape(16, LANES) for a in loaded], axis=0
                        )
                        for h in range(2)
                    ],
                    axis=1,
                )
                for q in range(NQ)
            ],
            axis=0,
        )
        done = dot3(wide, pair_hi, pair_lo)
        for q in range(NQ):
            for h in range(2):
                mixed[h * 32:(h + 1) * 32, q * LANES:(q + 1) * LANES] = done[
                    q * 32:(q + 1) * 32, h * LANES:(h + 1) * LANES
                ]
        temper = mixed[:, 0:LANES]
        vapour = mixed[:, LANES:2 * LANES]
        condense = jnp.maximum(vapour - 0.5 * jnp.exp(0.3 * temper), 0.0)
        mixed[:, 0:LANES] = jnp.where(lane64 < HL, temper + 0.5 * condense, temper)
        mixed[:, LANES:2 * LANES] = jnp.where(lane64 < HL, vapour - condense, vapour)
        ready = dot_rows(mixed[...], perm_t[...])
        for n, t in enumerate(turns):
            for h in range(2):
                for x in range(2):
                    at = h * 32 + n * 16 + x * 8
                    back[h * 2 + x, rows_of(t), :] = ready[at:at + 8]
        rate = jnp.where(lane64[0:32] < HL, condense[0:32], pltpu.roll(condense[32:64], HL, axis=1))
        for n, t in enumerate(turns):
            for x in range(2):
                rate_ref[block(x, t), :] = rate[n * 16 + x * 8:n * 16 + x * 8 + 8]
        for j in range(16):
            for c in (step * 2, step * 2 + 1):
                place, k = in_pair((4 - PAIRS[c]) % 4, j)
                if j == 0 and PAIRS[c] == 0:
                    pltpu.make_async_copy(both_x(back, l, here), both_x(mid2, l, here), back_recv.at[c]).start()
                    pltpu.make_async_copy(both_x(back, l, here), spare.at[1], back_send).start()
                    continue
                remote(
                    both_x(back, k, place), both_x(mid2, l, here), back_send, back_recv.at[c], (s, bx * 32 + place, k)
                ).start()

        if step == 0:
            tv_copy.wait_recv()
            whole = jnp.concatenate([tv[0], tv[1]], axis=1)
            both = dot3(whole, pair_hi, pair_lo)
            level = lax.rem(lane128, HL)
            total = jnp.zeros((COLS, LANES), F32)
            for lo_ in range(2):
                part = both[:, lo_ * LANES:(lo_ + 1) * LANES]
                vapour = pltpu.roll(part, HL, axis=1)
                condense = jnp.maximum(vapour - 0.5 * jnp.exp(0.3 * part), 0.0)
                heat = part + 0.5 * condense
                moist = vapour - condense
                w = (1.0 + (level + lo_ * HL).astype(F32) / LEV) / math.sqrt(LEV)
                total = total + jnp.where(lane128 < HL, w * (0.5 * heat + 0.5 * moist), 0.0)
            flux = jnp.sum(total.T, axis=0, keepdims=True)
            flux_out[...] = jnp.broadcast_to(flux, (8, LANES))
            flux_copy = remote(flux_out, flux_in, flux_send, flux_recv, (1 - s, b, l))
            flux_copy.start()
            sends.append(flux_copy)

    flux_copy.wait_recv()
    forcing = jnp.dot(flux_in[...], weigh, precision=HIGH, preferred_element_type=F32)
    forcing = sea * forcing[0:1]
    curves = calm + omix_ref[:, 0:1] * forcing
    curves_ref[...] = curves
    entry = jnp.broadcast_to(sea * curves[0:1], (8, LANES))
    sst_out[...] = lax.dot_general(
        entry, weigh, (((1,), (1,)), ((), ())), precision=HIGH, preferred_element_type=F32
    )
    sst_copies = [
        remote(sst_out, sst_in.at[l], sst_send.at[k], sst_recv.at[l], (1 - s, b, k)) for k in range(2)
    ]
    for c in sst_copies:
        c.start()

    for h in range(2):
        rows_ref[:, h * CH:(h + 1) * CH] = back[h * 2:h * 2 + 2].reshape(64, CH)

    def store(i, src, dst):
        c = pltpu.make_async_copy(src, dst, out_sems.at[i])
        c.start()
        return c

    stores = [store(0, rate_ref, rate_hbm), store(1, rows_ref, rows_hbm), store(2, curves_ref, curves_hbm)]


    def pass_rows(c):
        turned = lax.rem(pair + PAIRS[c], 4)
        arrived = mid2.at[:, rows_of(turned)]
        pltpu.make_async_copy(arrived, arrived, back_recv.at[c]).wait()
        for d in range(3):
            copy = remote(
                mid2.at[lax.rem(bx + d + 1, 4), rows_of(turned)], home.at[block(bx, turned)],
                home_send.at[c, d], home_recv.at[c, d], along_x[d],
            )
            copy.start()
            last.append(copy)
        copy = pltpu.make_async_copy(mid2.at[bx, rows_of(turned)], home.at[block(bx, turned)], home_stay.at[c])
        copy.start()
        stays.append(copy)

    last, stays = [], []
    for c in range(4):
        pass_rows(c)

    for k in range(2):
        remote(sst_out, sst_in.at[k], sst_send.at[k], sst_recv.at[k], (1 - s, b, k)).wait_recv()
    surface = sst_in[0] + sst_in[1]
    col = iota((8, LANES), 1)
    surface = jnp.where(col // NY == iota((8, LANES), 0), surface, 0.0)
    pick = jnp.where(lax.rem(iota((COLS, NY), 0), NY) == iota((COLS, NY), 1), F32(1), F32(0))
    sst_ref[...] = jnp.dot(surface, pick, precision=HIGH, preferred_element_type=F32)

    stores.append(store(3, sst_ref, sst_hbm))

    for c in stays:
        c.wait()
    for c in last:
        c.wait_recv()
    sends += last
    pltpu.make_async_copy(mid, came, go_send).wait()
    pltpu.make_async_copy(back, mid2, back_send).wait()
    for c in sends:
        c.wait_send()
    for c in sst_copies:
        c.wait_send()
    for c in stores:
        c.wait()


def hand_over(*refs):
    order_hbm, src, dst, order_ref, held, out_ref, sems = refs[0], refs[1:6], refs[6:11], refs[11], refs[12:17], refs[17], refs[18]
    loads = [pltpu.make_async_copy(src[i], held[i], sems.at[0, i]) for i in range(5)]
    order = pltpu.make_async_copy(order_hbm, order_ref, sems.at[0, 5])
    stores = [pltpu.make_async_copy(held[i] if i else out_ref, dst[i], sems.at[1, i]) for i in range(5)]
    order.start()
    for c in loads:
        c.start()
    order.wait()
    hot_t = jnp.where(iota((COLS, COLS), 0) == order_ref[...], F32(1), F32(0)).astype(BF16)
    loads[0].wait()
    out_ref[...] = pick_rows(hot_t, held[0][...])
    for i in range(5):
        if i:
            loads[i].wait()
        stores[i].start()
    for c in stores:
        c.wait()


def on_device(
    state, u_wind, v_wind, mixing, stretch_order, remap_index, remap_weight, land_sea, ocean_temp, ocean_mixing,
):
    hbm = pl.BlockSpec(memory_space=pltpu.HBM)
    dma = pltpu.SemaphoreType.DMA
    big = pltpu.VMEM((COLS, CH), F32)
    split = pltpu.VMEM((4, 32, CH), F32)
    scratch = [
        pltpu.VMEM((CH, CH), BF16), pltpu.VMEM((CH, CH), BF16),
        pltpu.VMEM((COLS, LANES), F32), pltpu.VMEM((COLS, LANES), F32),
        big, big, big,
        pltpu.VMEM((NX, CH), F32), pltpu.VMEM((NX, CH), F32),
        pltpu.VMEM((2, NY, CH), F32), pltpu.VMEM((2, NY, CH), F32),
        pltpu.VMEM((2, NX, CH), F32),
        pltpu.VMEM((2, 1, CH), F32), pltpu.VMEM((2, 1, CH), F32),
        big, split,
        pltpu.VMEM((2, COLS, LANES), F32),
        pltpu.VMEM((8, LANES), F32), pltpu.VMEM((8, LANES), F32),
        pltpu.VMEM((8, LANES), F32), pltpu.VMEM((2, 8, LANES), F32),
        split, pltpu.VMEM((64, CH), F32),
        pltpu.VMEM((2, 2, 1, CH), F32),
        dma((2, 2, 5)), dma((2, 2, 5)), dma, dma, dma, dma, dma((2,)), dma((2,)),
        dma, dma((4,)), dma, dma((4,)),
        split, split, pltpu.SemaphoreType.REGULAR,
        dma((4, 3, 2)), dma((4, 3, 2)), dma, dma((4, 3)), dma((4, 3)), dma((4,)),
    ]
    out_shape = [
            jax.ShapeDtypeStruct((COLS, CH), F32),
            jax.ShapeDtypeStruct((64, LEV), F32),
            jax.ShapeDtypeStruct((64, LEV * NF), F32),
            jax.ShapeDtypeStruct(ocean_temp.shape, F32),
            jax.ShapeDtypeStruct((NX, NY), F32),
    ]
    ins = (
        state.reshape(COLS, CH),
        u_wind.reshape(COLS, HL),
        v_wind.reshape(COLS, HL),
        mixing,
        stretch_order.reshape(1, COLS),
        remap_index.T,
        remap_weight.T,
        land_sea.reshape(1, COLS),
        ocean_temp,
        ocean_mixing,
    )
    held = [pltpu.VMEM(a.shape, a.dtype) for a in (*ins, *out_shape[1:])]
    outs = pl.pallas_call(
        window_kernel,
        out_shape=out_shape,
        in_specs=[hbm] * 10,
        out_specs=[hbm] * 5,
        scratch_shapes=[*held, dma((10,)), dma((4,)), *scratch],
        compiler_params=pltpu.CompilerParams(
            collective_id=0, has_side_effects=True, vmem_limit_bytes=56 * 2**20
        ),
        name="window",
    )(*ins)
    outs = pl.pallas_call(
        hand_over,
        out_shape=out_shape,
        in_specs=[hbm] * 6,
        out_specs=[hbm] * 5,
        scratch_shapes=[
            pltpu.VMEM((1, COLS), jnp.int32), *(pltpu.VMEM(a.shape, a.dtype) for a in out_shape), big, dma((2, 6))
        ],
        compiler_params=pltpu.CompilerParams(vmem_limit_bytes=56 * 2**20),
        name="outputs",
    )(ins[4], *outs)
    return (outs[0].reshape(state.shape), *outs[1:])


def solution(mesh):
    placed = (
        P("blk", "sec", "lev"),
        P("blk", "sec", "lev"),
        P("blk", "sec", "lev"),
        P(),
        P(("sec", "blk")),
        P(("sec", "blk", "lev"), None),
        P(("sec", "blk", "lev"), None),
        P(("sec", "blk", "lev")),
        P(None, ("sec", "blk", "lev")),
        P(),
    )
    return jax.shard_map(
        on_device,
        mesh=mesh,
        in_specs=placed,
        out_specs=(
            P("blk", "sec", "lev"),
            P(("sec", "blk", "lev"), None),
            P(("sec", "blk", "lev"), None),
            P(None, ("sec", "blk", "lev")),
            P("blk", "sec"),
        ),
        check_vma=False,
    )
```

```python
import functools
import math

import jax
import jax.numpy as jnp
import numpy as np
from jax import lax
from jax.experimental import pallas as pl
from jax.experimental.pallas import tpu as pltpu
from jax.sharding import PartitionSpec as P

NP = 4
LEV = 128
NF = 12
NX, NY = 8, 16
COLS = NX * NY
HL = 64
CH = HL * NF
NBLK = 128
LANES = 128
NQ = CH // LANES
PAIRS = (2, 0, 1, 3)
F32 = jnp.float32
BF16 = jnp.bfloat16
HIGH = lax.Precision.HIGHEST
MESH = pl.DeviceIdType.MESH


def gll_derivative():
    nodes = np.array([-1.0, -1.0 / math.sqrt(5.0), 1.0 / math.sqrt(5.0), 1.0])
    count = nodes.shape[0]
    bary = np.ones(count)
    for j in range(count):
        for k in range(count):
            if k != j:
                bary[j] = bary[j] / (nodes[j] - nodes[k])
    table = np.zeros((count, count))
    for i in range(count):
        for j in range(count):
            if i != j:
                table[i, j] = bary[j] / bary[i] / (nodes[i] - nodes[j])
        table[i, i] = -np.sum(table[i])
    return table.astype(np.float32)


def iota(shape, dim):
    return lax.broadcasted_iota(jnp.int32, shape, dim)


def split2(x):
    hi = x.astype(BF16)
    lo = (x - hi.astype(F32)).astype(BF16)
    return hi, lo


def dot(a, b):
    return jnp.dot(a, b, preferred_element_type=F32)


def dot3(a, b_hi, b_lo):
    hi, lo = split2(a)
    both = dot(jnp.concatenate([hi, lo], axis=0), b_hi)
    return both[:a.shape[0]] + both[a.shape[0]:] + dot(hi, b_lo)


def dot_rows(a, hot):
    both = dot(jnp.concatenate(split2(a), axis=0), hot)
    return both[:a.shape[0]] + both[a.shape[0]:]


def pick_rows(hot, a):
    return dot(jnp.concatenate([hot, hot], axis=1), jnp.concatenate(split2(a), axis=0))


def remote(src, dst, send, recv, device):
    return pltpu.make_async_remote_copy(
        src_ref=src, dst_ref=dst, send_sem=send, recv_sem=recv,
        device_id=device, device_id_type=MESH,
    )


def row(ref, r):
    return ref.at[pl.ds(r, 1)]


def advect(field_ref, uw_ref, vw_ref, out_ref, table, part):
    y8 = iota((8, LANES), 0)
    at = lax.rem(y8, NP)
    coefs = {}
    for d in range(-3, 4):
        c = jnp.zeros((8, LANES), F32)
        for i in range(NP):
            if 0 <= i + d < NP:
                c = jnp.where(at == i, F32(table[i, i + d]), c)
        coefs[d] = c[None]
    for q in range(part * 3, part * 3 + 3):
        lanes = slice(q * LANES, (q + 1) * LANES)
        for e in range(2):
            rows = slice(e * 64, (e + 1) * 64)
            f = field_ref[rows, lanes].reshape(NP, NY, LANES)
            dx = []
            for i in range(NP):
                acc = F32(table[i, 0]) * f[0]
                for j in range(1, NP):
                    acc = acc + F32(table[i, j]) * f[j]
                dx.append(acc[None])
            dx = jnp.concatenate(dx, axis=0).reshape(64, LANES)
            f8 = f.reshape(8, 8, LANES)
            dy = coefs[0] * f8
            for d in (-3, -2, -1, 1, 2, 3):
                dy = dy + coefs[d] * pltpu.roll(f8, (-d) % 8, axis=1)
            dy = dy.reshape(64, LANES)
            out_ref[rows, lanes] = f.reshape(64, LANES) - (
                uw_ref[rows, :] * dx + vw_ref[rows, :] * dy
            )


def average(a_ref, x_from_left, x_from_right, edge_ref, cor_l, cor_r, out_ref, s, part):
    y = iota((NY, LANES), 0)
    i = lax.rem(y, NP)
    at_edge = ((y == NY - 1) & (s == 0)) | ((y == 0) & (s == 1))
    closed = ((y == NY - 1) & (s == 1)) | ((y == 0) & (s == 0))
    inside = ((i == 0) | (i == NP - 1)) & jnp.logical_not(closed)
    for q in range(part * 3, part * 3 + 3):
        lanes = slice(q * LANES, (q + 1) * LANES)
        a = [a_ref[x * NY:(x + 1) * NY, lanes] for x in range(NX)]
        e = edge_ref[:, lanes]
        e = [e[x:x + 1] for x in range(NX)]
        a[0] = 0.5 * (a[0] + x_from_left[:, lanes])
        a[7] = 0.5 * (a[7] + x_from_right[:, lanes])
        a[3] = a[4] = 0.5 * (a[3] + a[4])
        e[0] = 0.5 * (e[0] + cor_l[0:1, lanes])
        e[7] = 0.5 * (e[7] + cor_r[0:1, lanes])
        e[3] = e[4] = 0.5 * (e[3] + e[4])
        for x in range(NX):
            f = a[x]
            up = pltpu.roll(f, NY - 1, axis=0)
            dn = pltpu.roll(f, 1, axis=0)
            nb = jnp.where(i == NP - 1, up, dn)
            nb = jnp.where(at_edge, jnp.broadcast_to(e[x], (NY, LANES)), nb)
            out_ref[x * NY:(x + 1) * NY, lanes] = jnp.where(inside, 0.5 * (f + nb), f)


def window_kernel(
    state_hbm, u_hbm, v_hbm, mixing_hbm, order_hbm, index_hbm, weight_hbm, sea_hbm, temp_hbm, omix_hbm,
    home, rate_hbm, rows_hbm, curves_hbm, sst_hbm,
    state_ref, u_ref, v_ref, mixing_ref, order_ref, index_ref, weight_ref, sea_ref, temp_ref, omix_ref,
    rate_ref, rows_ref, curves_ref, sst_ref, in_sems, out_sems,
    perm, perm_t, uw, vw, field, adv1, adv2, edge1, edge2, xl, xr, ye, cl, cr,
    gone, came, tv, flux_out, flux_in, sst_out, sst_in, back, mixed, spare,
    halo_send, halo_recv, tv_send, tv_recv, flux_send, flux_recv, sst_send, sst_recv,
    go_send, go_recv, back_send, back_recv,
    mid, mid2, plane, mid_send, mid_recv, stay_sem, home_send, home_recv, home_stay,
):
    s, b, l = lax.axis_index("sec"), lax.axis_index("blk"), lax.axis_index("lev")
    table = gll_derivative()
    left, right = lax.rem(b + NBLK - 1, NBLK), lax.rem(b + 1, NBLK)

    loads = [
        pltpu.make_async_copy(src, dst, in_sems.at[i])
        for i, (src, dst) in enumerate((
            (state_hbm, state_ref), (u_hbm, u_ref), (v_hbm, v_ref), (order_hbm, order_ref), (mixing_hbm, mixing_ref),
            (index_hbm, index_ref), (weight_hbm, weight_ref), (sea_hbm, sea_ref), (temp_hbm, temp_ref), (omix_hbm, omix_ref),
        ))
    ]
    for c in loads[:3]:
        c.start()

    barrier = pltpu.get_barrier_semaphore()

    def greet(device):
        pl.semaphore_signal(barrier, inc=1, device_id=device, device_id_type=MESH)

    bx, by, bz = b // 32, lax.rem(b // 4, 8), lax.rem(b, 4)
    pair = by // 2
    along_x = [(s, lax.rem(bx + d, 4) * 32 + lax.rem(b, 32), l) for d in range(1, 4)]
    along_y = [(s, bx * 32 + lax.rem(by + d, 8) * 4 + bz, l) for d in range(1, 8)]
    along_z = [(s, bx * 32 + by * 4 + lax.rem(bz + d, 4), l) for d in range(1, 4)]
    along_z += [(s, bx * 32 + by * 4 + lax.rem(bz + d, 4), 1 - l) for d in range(4)]
    near = [(s, left, l), (s, right, l), (1 - s, b, l), (1 - s, left, l), (1 - s, right, l), (1 - s, b, 1 - l)]
    near += along_x + along_z + along_y
    for device in near:
        greet(device)

    for c in loads[3:]:
        c.start()

    tall, wide = (CH, LANES), (1, LANES)
    for q in range(NQ):
        to = iota(wide, 1) + q * LANES
        perm[:, q * LANES:(q + 1) * LANES] = jnp.where(
            iota(tall, 0) == (to & (HL - 1)) * NF + (to >> 6), F32(1), F32(0)
        ).astype(BF16)
    for c in loads[:3]:
        c.wait()
    field[...] = dot_rows(state_ref[...], perm[...])
    for ref, wind in ((uw, u_ref), (vw, v_ref)):
        w = F32(0.1) * wind[...]
        ref[...] = jnp.concatenate([w, w], axis=1)


    sends = []

    def exchange(turn, part):
        a, edge = ((adv1, edge1), (adv2, edge2))[turn]
        lanes = slice(part * CH // 2, (part + 1) * CH // 2)
        cut = pl.ds(part * CH // 2, CH // 2)
        for x in range(NX):
            bottom, top = a[x * NY:x * NY + 1, lanes], a[(x + 1) * NY - 1:(x + 1) * NY, lanes]
            edge[x:x + 1, lanes] = jnp.where(s == 0, top, bottom)
        parts = (
            (a.at[pl.ds(0, NY), cut], xr.at[turn, :, cut], (s, left, l)),
            (a.at[pl.ds(COLS - NY, NY), cut], xl.at[turn, :, cut], (s, right, l)),
            (edge.at[:, cut], ye.at[turn, :, cut], (1 - s, b, l)),
            (edge.at[pl.ds(0, 1), cut], cr.at[turn, :, cut], (1 - s, left, l)),
            (edge.at[pl.ds(NX - 1, 1), cut], cl.at[turn, :, cut], (1 - s, right, l)),
        )
        copies = [
            remote(src, dst, halo_send.at[turn, part, i], halo_recv.at[turn, part, i], device)
            for i, (src, dst, device) in enumerate(parts)
        ]
        for c in copies:
            c.start()
        sends.extend(copies)
        return copies

    def settle(turn, part, copies):
        for c in copies:
            c.wait_recv()
        a = (adv1, adv2)[turn]
        average(a, xl.at[turn], xr.at[turn], ye.at[turn], cl.at[turn], cr.at[turn], field, s, part)

    for part in range(2):
        advect(field, uw, vw, adv1, table, part)
    pl.semaphore_wait(barrier, len(near))
    first = [exchange(0, part) for part in range(2)]
    for device in along_y:
        pl.semaphore_signal(plane, inc=1, device_id=device, device_id_type=MESH)
    source = iota(tall, 0)
    source = (source & (HL - 1)) * NF + (source >> 6)
    for q in range(NQ):
        perm_t[:, q * LANES:(q + 1) * LANES] = jnp.where(
            source == iota(wide, 1) + q * LANES, F32(1), F32(0)
        ).astype(BF16)
    for c in loads[3:]:
        c.wait()

    square = (COLS, COLS)
    hot_t = jnp.where(iota(square, 0) == order_ref[...], F32(1), F32(0))
    hot = hot_t.T.astype(BF16)

    mt = mixing_ref[...].T
    lane = iota((HL, LANES), 1)
    blocks = []
    for li in range(2):
        part = mt[li * HL:(li + 1) * HL]
        turned = pltpu.roll(part, HL, axis=1)
        zero = jnp.zeros_like(part)
        blocks.append(jnp.concatenate([jnp.where(lane < HL, part, zero), jnp.where(lane < HL, turned, zero)], axis=1))
        blocks.append(jnp.concatenate([jnp.where(lane < HL, zero, turned), jnp.where(lane < HL, zero, part)], axis=1))
    pair_hi, pair_lo = split2(jnp.concatenate(blocks, axis=0))

    sea = sea_ref[...].astype(F32)
    weigh = jnp.zeros(square, F32)
    for m in range(4):
        weigh = weigh + jnp.where(iota(square, 0) == index_ref[m:m + 1, :], weight_ref[m:m + 1, :], F32(0))
    calm = jnp.dot(omix_ref[...], temp_ref[...], precision=HIGH, preferred_element_type=F32)


    second = []
    for part in range(2):
        settle(0, part, first[part])
        advect(field, uw, vw, adv2, table, part)
        second.append(exchange(1, part))

    lane128 = iota((COLS, LANES), 1)
    here = by * 4 + bz

    def rows_of(turned):
        return pl.ds(pl.multiple_of(turned * 8, 8), 8)

    def block(x, turned):
        return pl.ds(pl.multiple_of(x * 32 + turned * 8, 8), 8)

    def in_pair(c, j):
        y = lax.rem(pair + c, 4) * 2 + lax.rem(by + j, 2)
        return y * 4 + lax.rem(bz + j // 4, 4), lax.rem(l + j // 2, 2)

    across = []
    for part in range(2):
        settle(1, part, second[part])
        if part == 0:
            tv[pl.ds(l, 1)] = jnp.where(
                lane128 < HL, field[:, 0:LANES], pltpu.roll(field[:, LANES:2 * LANES], HL, axis=1)
            )[None]
            tv_copy = remote(tv.at[l], tv.at[l], tv_send, tv_recv, (s, b, 1 - l))
            tv_copy.start()
            sends.append(tv_copy)
        lanes = slice(part * CH // 2, (part + 1) * CH // 2)
        cut = pl.ds(part * CH // 2, CH // 2)
        gone[:, lanes] = pick_rows(hot, field[:, lanes])
        for c in range(4):
            turned = lax.rem(pair + PAIRS[c], 4)
            for d in range(3):
                copy = remote(
                    gone.at[block(lax.rem(bx + d + 1, 4), turned), cut], mid.at[bx, rows_of(turned), cut],
                    mid_send.at[c, d, part], mid_recv.at[c, d, part], along_x[d],
                )
                copy.start()
                across.append((c, copy))
                sends.append(copy)
    stay = pltpu.make_async_copy(gone.at[pl.ds(pl.multiple_of(bx * 32, 32), 32)], mid.at[bx], stay_sem)
    stay.start()

    pl.semaphore_wait(plane, len(along_y))
    stay.wait()

    def both_x(ref, h, place):
        return ref.at[pl.ds(h * 2, 2), pl.ds(place, 1)]

    for c in range(4):
        for k, copy in across:
            if k == c:
                copy.wait_recv()

        def send_columns(j, carry, c=c):
            place, h = in_pair(PAIRS[c], j)
            remote(
                both_x(mid, h, place), both_x(came, l, here), go_send, go_recv.at[c], (s, bx * 32 + place, h)
            ).start()
            return carry

        lax.fori_loop(0 if PAIRS[c] else 1, 16, send_columns, 0, unroll=True)
        if PAIRS[c] == 0:
            pltpu.make_async_copy(both_x(mid, l, here), both_x(came, l, here), go_recv.at[c]).start()
            pltpu.make_async_copy(both_x(mid, l, here), spare.at[0], go_send).start()

    tv_copy.wait_recv()
    whole = jnp.concatenate([tv[0], tv[1]], axis=1)
    both = dot3(whole, pair_hi, pair_lo)
    level = lax.rem(lane128, HL)
    total = jnp.zeros((COLS, LANES), F32)
    for lo_ in range(2):
        part = both[:, lo_ * LANES:(lo_ + 1) * LANES]
        vapour = pltpu.roll(part, HL, axis=1)
        condense = jnp.maximum(vapour - 0.5 * jnp.exp(0.3 * part), 0.0)
        heat = part + 0.5 * condense
        moist = vapour - condense
        w = (1.0 + (level + lo_ * HL).astype(F32) / LEV) / math.sqrt(LEV)
        total = total + jnp.where(lane128 < HL, w * (0.5 * heat + 0.5 * moist), 0.0)
    flux = jnp.sum(total.T, axis=0, keepdims=True)
    flux_out[...] = jnp.broadcast_to(flux, (8, LANES))
    flux_copy = remote(flux_out, flux_in, flux_send, flux_recv, (1 - s, b, l))
    flux_copy.start()
    sends.append(flux_copy)

    lane64 = iota((64, LANES), 1)
    for step in range(2):
        turns = []
        for c in (step * 2, step * 2 + 1):
            turns.append(lax.rem(pair + 4 - PAIRS[c], 4))
            arrived = came.at[:, rows_of(turns[-1])]
            pltpu.make_async_copy(arrived, arrived, go_recv.at[c]).wait()
        loaded = [came[:, rows_of(t), :] for t in turns]
        wide = jnp.concatenate(
            [
                jnp.concatenate(
                    [
                        jnp.concatenate(
                            [a[h * 2:h * 2 + 2, :, q * LANES:(q + 1) * LANES].reshape(16, LANES) for a in loaded], axis=0
                        )
                        for h in range(2)
                    ],
                    axis=1,
                )
                for q in range(NQ)
            ],
            axis=0,
        )
        done = dot3(wide, pair_hi, pair_lo)
        for q in range(NQ):
            for h in range(2):
                mixed[h * 32:(h + 1) * 32, q * LANES:(q + 1) * LANES] = done[
                    q * 32:(q + 1) * 32, h * LANES:(h + 1) * LANES
                ]
        temper = mixed[:, 0:LANES]
        vapour = mixed[:, LANES:2 * LANES]
        condense = jnp.maximum(vapour - 0.5 * jnp.exp(0.3 * temper), 0.0)
        mixed[:, 0:LANES] = jnp.where(lane64 < HL, temper + 0.5 * condense, temper)
        mixed[:, LANES:2 * LANES] = jnp.where(lane64 < HL, vapour - condense, vapour)
        ready = dot_rows(mixed[...], perm_t[...])
        for n, t in enumerate(turns):
            for h in range(2):
                for x in range(2):
                    at = h * 32 + n * 16 + x * 8
                    back[h * 2 + x, rows_of(t), :] = ready[at:at + 8]
        rate = jnp.where(lane64[0:32] < HL, condense[0:32], pltpu.roll(condense[32:64], HL, axis=1))
        for n, t in enumerate(turns):
            for x in range(2):
                rate_ref[block(x, t), :] = rate[n * 16 + x * 8:n * 16 + x * 8 + 8]
        for j in range(16):
            for c in (step * 2, step * 2 + 1):
                place, k = in_pair((4 - PAIRS[c]) % 4, j)
                if j == 0 and PAIRS[c] == 0:
                    pltpu.make_async_copy(both_x(back, l, here), both_x(mid2, l, here), back_recv.at[c]).start()
                    pltpu.make_async_copy(both_x(back, l, here), spare.at[1], back_send).start()
                    continue
                remote(
                    both_x(back, k, place), both_x(mid2, l, here), back_send, back_recv.at[c], (s, bx * 32 + place, k)
                ).start()

    flux_copy.wait_recv()
    forcing = jnp.dot(flux_in[...], weigh, precision=HIGH, preferred_element_type=F32)
    forcing = sea * forcing[0:1]
    curves = calm + omix_ref[:, 0:1] * forcing
    curves_ref[...] = curves
    entry = jnp.broadcast_to(sea * curves[0:1], (8, LANES))
    sst_out[...] = lax.dot_general(
        entry, weigh, (((1,), (1,)), ((), ())), precision=HIGH, preferred_element_type=F32
    )
    sst_copies = [
        remote(sst_out, sst_in.at[l], sst_send.at[k], sst_recv.at[l], (1 - s, b, k)) for k in range(2)
    ]
    for c in sst_copies:
        c.start()

    for h in range(2):
        rows_ref[:, h * CH:(h + 1) * CH] = back[h * 2:h * 2 + 2].reshape(64, CH)

    def store(i, src, dst):
        c = pltpu.make_async_copy(src, dst, out_sems.at[i])
        c.start()
        return c

    stores = [store(0, rate_ref, rate_hbm), store(1, rows_ref, rows_hbm), store(2, curves_ref, curves_hbm)]


    def pass_rows(c):
        turned = lax.rem(pair + PAIRS[c], 4)
        arrived = mid2.at[:, rows_of(turned)]
        pltpu.make_async_copy(arrived, arrived, back_recv.at[c]).wait()
        for d in range(3):
            copy = remote(
                mid2.at[lax.rem(bx + d + 1, 4), rows_of(turned)], home.at[block(bx, turned)],
                home_send.at[c, d], home_recv.at[c, d], along_x[d],
            )
            copy.start()
            last.append(copy)
        copy = pltpu.make_async_copy(mid2.at[bx, rows_of(turned)], home.at[block(bx, turned)], home_stay.at[c])
        copy.start()
        stays.append(copy)

    last, stays = [], []
    for c in range(4):
        pass_rows(c)

    for k in range(2):
        remote(sst_out, sst_in.at[k], sst_send.at[k], sst_recv.at[k], (1 - s, b, k)).wait_recv()
    surface = sst_in[0] + sst_in[1]
    col = iota((8, LANES), 1)
    surface = jnp.where(col // NY == iota((8, LANES), 0), surface, 0.0)
    pick = jnp.where(lax.rem(iota((COLS, NY), 0), NY) == iota((COLS, NY), 1), F32(1), F32(0))
    sst_ref[...] = jnp.dot(surface, pick, precision=HIGH, preferred_element_type=F32)

    stores.append(store(3, sst_ref, sst_hbm))

    for c in stays:
        c.wait()
    for c in last:
        c.wait_recv()
    sends += last
    pltpu.make_async_copy(mid, came, go_send).wait()
    pltpu.make_async_copy(back, mid2, back_send).wait()
    for c in sends:
        c.wait_send()
    for c in sst_copies:
        c.wait_send()
    for c in stores:
        c.wait()


def hand_over(*refs):
    order_hbm, src, dst, order_ref, held, out_ref, sems = refs[0], refs[1:6], refs[6:11], refs[11], refs[12:17], refs[17], refs[18]
    loads = [pltpu.make_async_copy(src[i], held[i], sems.at[0, i]) for i in range(5)]
    order = pltpu.make_async_copy(order_hbm, order_ref, sems.at[0, 5])
    stores = [pltpu.make_async_copy(held[i] if i else out_ref, dst[i], sems.at[1, i]) for i in range(5)]
    order.start()
    for c in loads:
        c.start()
    order.wait()
    hot_t = jnp.where(iota((COLS, COLS), 0) == order_ref[...], F32(1), F32(0)).astype(BF16)
    loads[0].wait()
    out_ref[...] = pick_rows(hot_t, held[0][...])
    for i in range(5):
        if i:
            loads[i].wait()
        stores[i].start()
    for c in stores:
        c.wait()


def on_device(
    state, u_wind, v_wind, mixing, stretch_order, remap_index, remap_weight, land_sea, ocean_temp, ocean_mixing,
):
    hbm = pl.BlockSpec(memory_space=pltpu.HBM)
    dma = pltpu.SemaphoreType.DMA
    big = pltpu.VMEM((COLS, CH), F32)
    split = pltpu.VMEM((4, 32, CH), F32)
    scratch = [
        pltpu.VMEM((CH, CH), BF16), pltpu.VMEM((CH, CH), BF16),
        pltpu.VMEM((COLS, LANES), F32), pltpu.VMEM((COLS, LANES), F32),
        big, big, big,
        pltpu.VMEM((NX, CH), F32), pltpu.VMEM((NX, CH), F32),
        pltpu.VMEM((2, NY, CH), F32), pltpu.VMEM((2, NY, CH), F32),
        pltpu.VMEM((2, NX, CH), F32),
        pltpu.VMEM((2, 1, CH), F32), pltpu.VMEM((2, 1, CH), F32),
        big, split,
        pltpu.VMEM((2, COLS, LANES), F32),
        pltpu.VMEM((8, LANES), F32), pltpu.VMEM((8, LANES), F32),
        pltpu.VMEM((8, LANES), F32), pltpu.VMEM((2, 8, LANES), F32),
        split, pltpu.VMEM((64, CH), F32),
        pltpu.VMEM((2, 2, 1, CH), F32),
        dma((2, 2, 5)), dma((2, 2, 5)), dma, dma, dma, dma, dma((2,)), dma((2,)),
        dma, dma((4,)), dma, dma((4,)),
        split, split, pltpu.SemaphoreType.REGULAR,
        dma((4, 3, 2)), dma((4, 3, 2)), dma, dma((4, 3)), dma((4, 3)), dma((4,)),
    ]
    out_shape = [
            jax.ShapeDtypeStruct((COLS, CH), F32),
            jax.ShapeDtypeStruct((64, LEV), F32),
            jax.ShapeDtypeStruct((64, LEV * NF), F32),
            jax.ShapeDtypeStruct(ocean_temp.shape, F32),
            jax.ShapeDtypeStruct((NX, NY), F32),
    ]
    ins = (
        state.reshape(COLS, CH),
        u_wind.reshape(COLS, HL),
        v_wind.reshape(COLS, HL),
        mixing,
        stretch_order.reshape(1, COLS),
        remap_index.T,
        remap_weight.T,
        land_sea.reshape(1, COLS),
        ocean_temp,
        ocean_mixing,
    )
    held = [pltpu.VMEM(a.shape, a.dtype) for a in (*ins, *out_shape[1:])]
    outs = pl.pallas_call(
        window_kernel,
        out_shape=out_shape,
        in_specs=[hbm] * 10,
        out_specs=[hbm] * 5,
        scratch_shapes=[*held, dma((10,)), dma((4,)), *scratch],
        compiler_params=pltpu.CompilerParams(
            collective_id=0, has_side_effects=True, vmem_limit_bytes=56 * 2**20
        ),
        name="window",
    )(*ins)
    outs = pl.pallas_call(
        hand_over,
        out_shape=out_shape,
        in_specs=[hbm] * 6,
        out_specs=[hbm] * 5,
        scratch_shapes=[
            pltpu.VMEM((1, COLS), jnp.int32), *(pltpu.VMEM(a.shape, a.dtype) for a in out_shape), big, dma((2, 6))
        ],
        compiler_params=pltpu.CompilerParams(vmem_limit_bytes=56 * 2**20),
        name="outputs",
    )(ins[4], *outs)
    return (outs[0].reshape(state.shape), *outs[1:])


def solution(mesh):
    placed = (
        P("blk", "sec", "lev"),
        P("blk", "sec", "lev"),
        P("blk", "sec", "lev"),
        P(),
        P(("sec", "blk")),
        P(("sec", "blk", "lev"), None),
        P(("sec", "blk", "lev"), None),
        P(("sec", "blk", "lev")),
        P(None, ("sec", "blk", "lev")),
        P(),
    )
    return jax.shard_map(
        on_device,
        mesh=mesh,
        in_specs=placed,
        out_specs=(
            P("blk", "sec", "lev"),
            P(("sec", "blk", "lev"), None),
            P(("sec", "blk", "lev"), None),
            P(None, ("sec", "blk", "lev")),
            P("blk", "sec"),
        ),
        check_vma=False,
    )
```

```python
import functools
import math

import jax
import jax.numpy as jnp
import numpy as np
from jax import lax
from jax.experimental import pallas as pl
from jax.experimental.pallas import tpu as pltpu
from jax.sharding import PartitionSpec as P

NP = 4
LEV = 128
NF = 12
NX, NY = 8, 16
COLS = NX * NY
HL = 64
CH = HL * NF
NBLK = 128
LANES = 128
NQ = CH // LANES
PAIRS = (2, 0, 1, 3)
F32 = jnp.float32
BF16 = jnp.bfloat16
HIGH = lax.Precision.HIGHEST
MESH = pl.DeviceIdType.MESH


def gll_derivative():
    nodes = np.array([-1.0, -1.0 / math.sqrt(5.0), 1.0 / math.sqrt(5.0), 1.0])
    count = nodes.shape[0]
    bary = np.ones(count)
    for j in range(count):
        for k in range(count):
            if k != j:
                bary[j] = bary[j] / (nodes[j] - nodes[k])
    table = np.zeros((count, count))
    for i in range(count):
        for j in range(count):
            if i != j:
                table[i, j] = bary[j] / bary[i] / (nodes[i] - nodes[j])
        table[i, i] = -np.sum(table[i])
    return table.astype(np.float32)


def iota(shape, dim):
    return lax.broadcasted_iota(jnp.int32, shape, dim)


def split2(x):
    hi = x.astype(BF16)
    lo = (x - hi.astype(F32)).astype(BF16)
    return hi, lo


def dot(a, b):
    return jnp.dot(a, b, preferred_element_type=F32)


def dot3(a, b_hi, b_lo):
    hi, lo = split2(a)
    both = dot(jnp.concatenate([hi, lo], axis=0), b_hi)
    return both[:a.shape[0]] + both[a.shape[0]:] + dot(hi, b_lo)


def dot_rows(a, hot):
    both = dot(jnp.concatenate(split2(a), axis=0), hot)
    return both[:a.shape[0]] + both[a.shape[0]:]


def pick_rows(hot, a):
    return dot(jnp.concatenate([hot, hot], axis=1), jnp.concatenate(split2(a), axis=0))


def remote(src, dst, send, recv, device):
    return pltpu.make_async_remote_copy(
        src_ref=src, dst_ref=dst, send_sem=send, recv_sem=recv,
        device_id=device, device_id_type=MESH,
    )


def row(ref, r):
    return ref.at[pl.ds(r, 1)]


def advect(field_ref, uw_ref, vw_ref, out_ref, table, part):
    y8 = iota((8, LANES), 0)
    at = lax.rem(y8, NP)
    coefs = {}
    for d in range(-3, 4):
        c = jnp.zeros((8, LANES), F32)
        for i in range(NP):
            if 0 <= i + d < NP:
                c = jnp.where(at == i, F32(table[i, i + d]), c)
        coefs[d] = c[None]
    for q in range(part * 3, part * 3 + 3):
        lanes = slice(q * LANES, (q + 1) * LANES)
        for e in range(2):
            rows = slice(e * 64, (e + 1) * 64)
            f = field_ref[rows, lanes].reshape(NP, NY, LANES)
            dx = []
            for i in range(NP):
                acc = F32(table[i, 0]) * f[0]
                for j in range(1, NP):
                    acc = acc + F32(table[i, j]) * f[j]
                dx.append(acc[None])
            dx = jnp.concatenate(dx, axis=0).reshape(64, LANES)
            f8 = f.reshape(8, 8, LANES)
            dy = coefs[0] * f8
            for d in (-3, -2, -1, 1, 2, 3):
                dy = dy + coefs[d] * pltpu.roll(f8, (-d) % 8, axis=1)
            dy = dy.reshape(64, LANES)
            out_ref[rows, lanes] = f.reshape(64, LANES) - (
                uw_ref[rows, :] * dx + vw_ref[rows, :] * dy
            )


def average(a_ref, x_from_left, x_from_right, edge_ref, cor_l, cor_r, out_ref, s, part):
    y = iota((NY, LANES), 0)
    i = lax.rem(y, NP)
    at_edge = ((y == NY - 1) & (s == 0)) | ((y == 0) & (s == 1))
    closed = ((y == NY - 1) & (s == 1)) | ((y == 0) & (s == 0))
    inside = ((i == 0) | (i == NP - 1)) & jnp.logical_not(closed)
    for q in range(part * 3, part * 3 + 3):
        lanes = slice(q * LANES, (q + 1) * LANES)
        a = [a_ref[x * NY:(x + 1) * NY, lanes] for x in range(NX)]
        e = edge_ref[:, lanes]
        e = [e[x:x + 1] for x in range(NX)]
        a[0] = 0.5 * (a[0] + x_from_left[:, lanes])
        a[7] = 0.5 * (a[7] + x_from_right[:, lanes])
        a[3] = a[4] = 0.5 * (a[3] + a[4])
        e[0] = 0.5 * (e[0] + cor_l[0:1, lanes])
        e[7] = 0.5 * (e[7] + cor_r[0:1, lanes])
        e[3] = e[4] = 0.5 * (e[3] + e[4])
        for x in range(NX):
            f = a[x]
            up = pltpu.roll(f, NY - 1, axis=0)
            dn = pltpu.roll(f, 1, axis=0)
            nb = jnp.where(i == NP - 1, up, dn)
            nb = jnp.where(at_edge, jnp.broadcast_to(e[x], (NY, LANES)), nb)
            out_ref[x * NY:(x + 1) * NY, lanes] = jnp.where(inside, 0.5 * (f + nb), f)


def window_kernel(
    state_hbm, u_hbm, v_hbm, mixing_hbm, order_hbm, index_hbm, weight_hbm, sea_hbm, temp_hbm, omix_hbm,
    home, rate_hbm, rows_hbm, curves_hbm, sst_hbm,
    state_ref, u_ref, v_ref, mixing_ref, order_ref, index_ref, weight_ref, sea_ref, temp_ref, omix_ref,
    rate_ref, rows_ref, curves_ref, sst_ref, in_sems, out_sems,
    perm, perm_t, uw, vw, field, adv1, adv2, edge1, edge2, xl, xr, ye, cl, cr,
    gone, came, tv, flux_out, flux_in, sst_out, sst_in, back, mixed, spare,
    halo_send, halo_recv, tv_send, tv_recv, flux_send, flux_recv, sst_send, sst_recv,
    go_send, go_recv, back_send, back_recv,
    mid, mid2, plane, mid_send, mid_recv, stay_sem, home_send, home_recv, home_stay,
):
    s, b, l = lax.axis_index("sec"), lax.axis_index("blk"), lax.axis_index("lev")
    table = gll_derivative()
    left, right = lax.rem(b + NBLK - 1, NBLK), lax.rem(b + 1, NBLK)

    loads = [
        pltpu.make_async_copy(src, dst, in_sems.at[i])
        for i, (src, dst) in enumerate((
            (state_hbm, state_ref), (u_hbm, u_ref), (v_hbm, v_ref), (order_hbm, order_ref), (mixing_hbm, mixing_ref),
            (index_hbm, index_ref), (weight_hbm, weight_ref), (sea_hbm, sea_ref), (temp_hbm, temp_ref), (omix_hbm, omix_ref),
        ))
    ]
    for c in loads[:3]:
        c.start()

    barrier = pltpu.get_barrier_semaphore()

    def greet(device):
        pl.semaphore_signal(barrier, inc=1, device_id=device, device_id_type=MESH)

    bx, by, bz = b // 32, lax.rem(b // 4, 8), lax.rem(b, 4)
    pair = by // 2
    along_x = [(s, lax.rem(bx + d, 4) * 32 + lax.rem(b, 32), l) for d in range(1, 4)]
    along_y = [(s, bx * 32 + lax.rem(by + d, 8) * 4 + bz, l) for d in range(1, 8)]
    along_z = [(s, bx * 32 + by * 4 + lax.rem(bz + d, 4), l) for d in range(1, 4)]
    along_z += [(s, bx * 32 + by * 4 + lax.rem(bz + d, 4), 1 - l) for d in range(4)]
    near = [(s, left, l), (s, right, l), (1 - s, b, l), (1 - s, left, l), (1 - s, right, l), (1 - s, b, 1 - l)]
    near += along_x + along_z + along_y
    for device in near:
        greet(device)

    for c in loads[3:]:
        c.start()

    tall, wide = (CH, LANES), (1, LANES)
    for q in range(NQ):
        to = iota(wide, 1) + q * LANES
        perm[:, q * LANES:(q + 1) * LANES] = jnp.where(
            iota(tall, 0) == (to & (HL - 1)) * NF + (to >> 6), F32(1), F32(0)
        ).astype(BF16)
    for c in loads[:3]:
        c.wait()
    field[...] = dot_rows(state_ref[...], perm[...])
    for ref, wind in ((uw, u_ref), (vw, v_ref)):
        w = F32(0.1) * wind[...]
        ref[...] = jnp.concatenate([w, w], axis=1)


    sends = []

    def exchange(turn, part):
        a, edge = ((adv1, edge1), (adv2, edge2))[turn]
        lanes = slice(part * CH // 2, (part + 1) * CH // 2)
        cut = pl.ds(part * CH // 2, CH // 2)
        for x in range(NX):
            bottom, top = a[x * NY:x * NY + 1, lanes], a[(x + 1) * NY - 1:(x + 1) * NY, lanes]
            edge[x:x + 1, lanes] = jnp.where(s == 0, top, bottom)
        parts = (
            (a.at[pl.ds(0, NY), cut], xr.at[turn, :, cut], (s, left, l)),
            (a.at[pl.ds(COLS - NY, NY), cut], xl.at[turn, :, cut], (s, right, l)),
            (edge.at[:, cut], ye.at[turn, :, cut], (1 - s, b, l)),
            (edge.at[pl.ds(0, 1), cut], cr.at[turn, :, cut], (1 - s, left, l)),
            (edge.at[pl.ds(NX - 1, 1), cut], cl.at[turn, :, cut], (1 - s, right, l)),
        )
        copies = [
            remote(src, dst, halo_send.at[turn, part, i], halo_recv.at[turn, part, i], device)
            for i, (src, dst, device) in enumerate(parts)
        ]
        for c in copies:
            c.start()
        sends.extend(copies)
        return copies

    def settle(turn, part, copies):
        for c in copies:
            c.wait_recv()
        a = (adv1, adv2)[turn]
        average(a, xl.at[turn], xr.at[turn], ye.at[turn], cl.at[turn], cr.at[turn], field, s, part)

    for part in range(2):
        advect(field, uw, vw, adv1, table, part)
    pl.semaphore_wait(barrier, len(near))
    first = [exchange(0, part) for part in range(2)]
    for device in along_y:
        pl.semaphore_signal(plane, inc=1, device_id=device, device_id_type=MESH)
    source = iota(tall, 0)
    source = (source & (HL - 1)) * NF + (source >> 6)
    for q in range(NQ):
        perm_t[:, q * LANES:(q + 1) * LANES] = jnp.where(
            source == iota(wide, 1) + q * LANES, F32(1), F32(0)
        ).astype(BF16)
    for c in loads[3:]:
        c.wait()

    square = (COLS, COLS)
    hot_t = jnp.where(iota(square, 0) == order_ref[...], F32(1), F32(0))
    hot = hot_t.T.astype(BF16)

    mt = mixing_ref[...].T
    lane = iota((HL, LANES), 1)
    blocks = []
    for li in range(2):
        part = mt[li * HL:(li + 1) * HL]
        turned = pltpu.roll(part, HL, axis=1)
        zero = jnp.zeros_like(part)
        blocks.append(jnp.concatenate([jnp.where(lane < HL, part, zero), jnp.where(lane < HL, turned, zero)], axis=1))
        blocks.append(jnp.concatenate([jnp.where(lane < HL, zero, turned), jnp.where(lane < HL, zero, part)], axis=1))
    pair_hi, pair_lo = split2(jnp.concatenate(blocks, axis=0))

    sea = sea_ref[...].astype(F32)
    weigh = jnp.zeros(square, F32)
    for m in range(4):
        weigh = weigh + jnp.where(iota(square, 0) == index_ref[m:m + 1, :], weight_ref[m:m + 1, :], F32(0))
    calm = jnp.dot(omix_ref[...], temp_ref[...], precision=HIGH, preferred_element_type=F32)


    second = []
    for part in range(2):
        settle(0, part, first[part])
        advect(field, uw, vw, adv2, table, part)
        second.append(exchange(1, part))

    lane128 = iota((COLS, LANES), 1)
    here = by * 4 + bz

    def rows_of(turned):
        return pl.ds(pl.multiple_of(turned * 8, 8), 8)

    def block(x, turned):
        return pl.ds(pl.multiple_of(x * 32 + turned * 8, 8), 8)

    def in_pair(c, j):
        y = lax.rem(pair + c, 4) * 2 + lax.rem(by + j, 2)
        return y * 4 + lax.rem(bz + j // 4, 4), lax.rem(l + j // 2, 2)

    across = []
    for part in range(2):
        settle(1, part, second[part])
        if part == 0:
            tv[pl.ds(l, 1)] = jnp.where(
                lane128 < HL, field[:, 0:LANES], pltpu.roll(field[:, LANES:2 * LANES], HL, axis=1)
            )[None]
            tv_copy = remote(tv.at[l], tv.at[l], tv_send, tv_recv, (s, b, 1 - l))
            tv_copy.start()
            sends.append(tv_copy)
        lanes = slice(part * CH // 2, (part + 1) * CH // 2)
        cut = pl.ds(part * CH // 2, CH // 2)
        gone[:, lanes] = pick_rows(hot, field[:, lanes])
        for c in range(4):
            turned = lax.rem(pair + PAIRS[c], 4)
            for d in range(3):
                copy = remote(
                    gone.at[block(lax.rem(bx + d + 1, 4), turned), cut], mid.at[bx, rows_of(turned), cut],
                    mid_send.at[c, d, part], mid_recv.at[c, d, part], along_x[d],
                )
                copy.start()
                across.append((c, copy))
                sends.append(copy)
    stay = pltpu.make_async_copy(gone.at[pl.ds(pl.multiple_of(bx * 32, 32), 32)], mid.at[bx], stay_sem)
    stay.start()

    pl.semaphore_wait(plane, len(along_y))
    stay.wait()

    def both_x(ref, h, place):
        return ref.at[pl.ds(h * 2, 2), pl.ds(place, 1)]

    for c in range(4):
        for k, copy in across:
            if k == c:
                copy.wait_recv()

        def send_columns(j, carry, c=c):
            place, h = in_pair(PAIRS[c], j)
            remote(
                both_x(mid, h, place), both_x(came, l, here), go_send, go_recv.at[c], (s, bx * 32 + place, h)
            ).start()
            return carry

        lax.fori_loop(0 if PAIRS[c] else 1, 16, send_columns, 0, unroll=True)
        if PAIRS[c] == 0:
            pltpu.make_async_copy(both_x(mid, l, here), both_x(came, l, here), go_recv.at[c]).start()
            pltpu.make_async_copy(both_x(mid, l, here), spare.at[0], go_send).start()

    tv_copy.wait_recv()
    whole = jnp.concatenate([tv[0], tv[1]], axis=1)
    both = dot3(whole, pair_hi, pair_lo)
    level = lax.rem(lane128, HL)
    total = jnp.zeros((COLS, LANES), F32)
    for lo_ in range(2):
        part = both[:, lo_ * LANES:(lo_ + 1) * LANES]
        vapour = pltpu.roll(part, HL, axis=1)
        condense = jnp.maximum(vapour - 0.5 * jnp.exp(0.3 * part), 0.0)
        heat = part + 0.5 * condense
        moist = vapour - condense
        w = (1.0 + (level + lo_ * HL).astype(F32) / LEV) / math.sqrt(LEV)
        total = total + jnp.where(lane128 < HL, w * (0.5 * heat + 0.5 * moist), 0.0)
    flux = jnp.sum(total.T, axis=0, keepdims=True)
    flux_out[...] = jnp.broadcast_to(flux, (8, LANES))
    flux_copy = remote(flux_out, flux_in, flux_send, flux_recv, (1 - s, b, l))
    flux_copy.start()
    sends.append(flux_copy)

    lane64 = iota((64, LANES), 1)
    for step in range(2):
        turns = []
        for c in (step * 2, step * 2 + 1):
            turns.append(lax.rem(pair + 4 - PAIRS[c], 4))
            arrived = came.at[:, rows_of(turns[-1])]
            pltpu.make_async_copy(arrived, arrived, go_recv.at[c]).wait()
        loaded = [came[:, rows_of(t), :] for t in turns]
        wide = jnp.concatenate(
            [
                jnp.concatenate(
                    [
                        jnp.concatenate(
                            [a[h * 2:h * 2 + 2, :, q * LANES:(q + 1) * LANES].reshape(16, LANES) for a in loaded], axis=0
                        )
                        for h in range(2)
                    ],
                    axis=1,
                )
                for q in range(NQ)
            ],
            axis=0,
        )
        done = dot3(wide, pair_hi, pair_lo)
        for q in range(NQ):
            for h in range(2):
                mixed[h * 32:(h + 1) * 32, q * LANES:(q + 1) * LANES] = done[
                    q * 32:(q + 1) * 32, h * LANES:(h + 1) * LANES
                ]
        temper = mixed[:, 0:LANES]
        vapour = mixed[:, LANES:2 * LANES]
        condense = jnp.maximum(vapour - 0.5 * jnp.exp(0.3 * temper), 0.0)
        mixed[:, 0:LANES] = jnp.where(lane64 < HL, temper + 0.5 * condense, temper)
        mixed[:, LANES:2 * LANES] = jnp.where(lane64 < HL, vapour - condense, vapour)
        ready = dot_rows(mixed[...], perm_t[...])
        for n, t in enumerate(turns):
            for h in range(2):
                for x in range(2):
                    at = h * 32 + n * 16 + x * 8
                    back[h * 2 + x, rows_of(t), :] = ready[at:at + 8]
        rate = jnp.where(lane64[0:32] < HL, condense[0:32], pltpu.roll(condense[32:64], HL, axis=1))
        for n, t in enumerate(turns):
            for x in range(2):
                rate_ref[block(x, t), :] = rate[n * 16 + x * 8:n * 16 + x * 8 + 8]
        for j in range(16):
            for c in (step * 2, step * 2 + 1):
                place, k = in_pair((4 - PAIRS[c]) % 4, j)
                if j == 0 and PAIRS[c] == 0:
                    pltpu.make_async_copy(both_x(back, l, here), both_x(mid2, l, here), back_recv.at[c]).start()
                    pltpu.make_async_copy(both_x(back, l, here), spare.at[1], back_send).start()
                    continue
                remote(
                    both_x(back, k, place), both_x(mid2, l, here), back_send, back_recv.at[c], (s, bx * 32 + place, k)
                ).start()

    flux_copy.wait_recv()
    forcing = jnp.dot(flux_in[...], weigh, precision=HIGH, preferred_element_type=F32)
    forcing = sea * forcing[0:1]
    curves = calm + omix_ref[:, 0:1] * forcing
    curves_ref[...] = curves
    entry = jnp.broadcast_to(sea * curves[0:1], (8, LANES))
    sst_out[...] = lax.dot_general(
        entry, weigh, (((1,), (1,)), ((), ())), precision=HIGH, preferred_element_type=F32
    )
    sst_copies = [
        remote(sst_out, sst_in.at[l], sst_send.at[k], sst_recv.at[l], (1 - s, b, k)) for k in range(2)
    ]
    for c in sst_copies:
        c.start()

    for h in range(2):
        rows_ref[:, h * CH:(h + 1) * CH] = back[h * 2:h * 2 + 2].reshape(64, CH)

    def store(i, src, dst):
        c = pltpu.make_async_copy(src, dst, out_sems.at[i])
        c.start()
        return c

    stores = [store(0, rate_ref, rate_hbm), store(1, rows_ref, rows_hbm), store(2, curves_ref, curves_hbm)]


    def pass_rows(c):
        turned = lax.rem(pair + PAIRS[c], 4)
        arrived = mid2.at[:, rows_of(turned)]
        pltpu.make_async_copy(arrived, arrived, back_recv.at[c]).wait()
        for d in range(3):
            copy = remote(
                mid2.at[lax.rem(bx + d + 1, 4), rows_of(turned)], home.at[block(bx, turned)],
                home_send.at[c, d], home_recv.at[c, d], along_x[d],
            )
            copy.start()
            last.append(copy)
        copy = pltpu.make_async_copy(mid2.at[bx, rows_of(turned)], home.at[block(bx, turned)], home_stay.at[c])
        copy.start()
        stays.append(copy)

    last, stays = [], []
    for c in range(4):
        pass_rows(c)

    for k in range(2):
        remote(sst_out, sst_in.at[k], sst_send.at[k], sst_recv.at[k], (1 - s, b, k)).wait_recv()
    surface = sst_in[0] + sst_in[1]
    col = iota((8, LANES), 1)
    surface = jnp.where(col // NY == iota((8, LANES), 0), surface, 0.0)
    pick = jnp.where(lax.rem(iota((COLS, NY), 0), NY) == iota((COLS, NY), 1), F32(1), F32(0))
    sst_ref[...] = jnp.dot(surface, pick, precision=HIGH, preferred_element_type=F32)

    stores.append(store(3, sst_ref, sst_hbm))

    for c in stays:
        c.wait()
    for c in last:
        c.wait_recv()
    sends += last
    pltpu.make_async_copy(mid, came, go_send).wait()
    pltpu.make_async_copy(back, mid2, back_send).wait()
    for c in sends:
        c.wait_send()
    for c in sst_copies:
        c.wait_send()
    for c in stores:
        c.wait()


def hand_over(*refs):
    order_hbm, src, dst, order_ref, held, out_ref, sems = refs[0], refs[1:6], refs[6:11], refs[11], refs[12:17], refs[17], refs[18]
    cuts = [pl.ds(i * CH // 3, CH // 3) for i in range(3)]
    order = pltpu.make_async_copy(order_hbm, order_ref, sems.at[0, 0])
    loads = [pltpu.make_async_copy(src[0].at[:, cut], held[0].at[:, cut], sems.at[0, 5 + i]) for i, cut in enumerate(cuts)]
    stores = [pltpu.make_async_copy(out_ref.at[:, cut], dst[0].at[:, cut], sems.at[1, 5 + i]) for i, cut in enumerate(cuts)]
    others = [pltpu.make_async_copy(src[i], held[i], sems.at[0, i]) for i in range(1, 5)]
    results = [pltpu.make_async_copy(held[i], dst[i], sems.at[1, i]) for i in range(1, 5)]
    order.start()
    for c in loads + others:
        c.start()
    order.wait()
    hot_t = jnp.where(iota((COLS, COLS), 0) == order_ref[...], F32(1), F32(0)).astype(BF16)
    for i in range(3):
        loads[i].wait()
        lanes = slice(i * CH // 3, (i + 1) * CH // 3)
        out_ref[:, lanes] = pick_rows(hot_t, held[0][:, lanes])
        stores[i].start()
    for a, b in zip(others, results):
        a.wait()
        b.start()
    for c in stores + results:
        c.wait()


def on_device(
    state, u_wind, v_wind, mixing, stretch_order, remap_index, remap_weight, land_sea, ocean_temp, ocean_mixing,
):
    hbm = pl.BlockSpec(memory_space=pltpu.HBM)
    dma = pltpu.SemaphoreType.DMA
    big = pltpu.VMEM((COLS, CH), F32)
    split = pltpu.VMEM((4, 32, CH), F32)
    scratch = [
        pltpu.VMEM((CH, CH), BF16), pltpu.VMEM((CH, CH), BF16),
        pltpu.VMEM((COLS, LANES), F32), pltpu.VMEM((COLS, LANES), F32),
        big, big, big,
        pltpu.VMEM((NX, CH), F32), pltpu.VMEM((NX, CH), F32),
        pltpu.VMEM((2, NY, CH), F32), pltpu.VMEM((2, NY, CH), F32),
        pltpu.VMEM((2, NX, CH), F32),
        pltpu.VMEM((2, 1, CH), F32), pltpu.VMEM((2, 1, CH), F32),
        big, split,
        pltpu.VMEM((2, COLS, LANES), F32),
        pltpu.VMEM((8, LANES), F32), pltpu.VMEM((8, LANES), F32),
        pltpu.VMEM((8, LANES), F32), pltpu.VMEM((2, 8, LANES), F32),
        split, pltpu.VMEM((64, CH), F32),
        pltpu.VMEM((2, 2, 1, CH), F32),
        dma((2, 2, 5)), dma((2, 2, 5)), dma, dma, dma, dma, dma((2,)), dma((2,)),
        dma, dma((4,)), dma, dma((4,)),
        split, split, pltpu.SemaphoreType.REGULAR,
        dma((4, 3, 2)), dma((4, 3, 2)), dma, dma((4, 3)), dma((4, 3)), dma((4,)),
    ]
    out_shape = [
            jax.ShapeDtypeStruct((COLS, CH), F32),
            jax.ShapeDtypeStruct((64, LEV), F32),
            jax.ShapeDtypeStruct((64, LEV * NF), F32),
            jax.ShapeDtypeStruct(ocean_temp.shape, F32),
            jax.ShapeDtypeStruct((NX, NY), F32),
    ]
    ins = (
        state.reshape(COLS, CH),
        u_wind.reshape(COLS, HL),
        v_wind.reshape(COLS, HL),
        mixing,
        stretch_order.reshape(1, COLS),
        remap_index.T,
        remap_weight.T,
        land_sea.reshape(1, COLS),
        ocean_temp,
        ocean_mixing,
    )
    held = [pltpu.VMEM(a.shape, a.dtype) for a in (*ins, *out_shape[1:])]
    outs = pl.pallas_call(
        window_kernel,
        out_shape=out_shape,
        in_specs=[hbm] * 10,
        out_specs=[hbm] * 5,
        scratch_shapes=[*held, dma((10,)), dma((4,)), *scratch],
        compiler_params=pltpu.CompilerParams(
            collective_id=0, has_side_effects=True, vmem_limit_bytes=56 * 2**20
        ),
        name="window",
    )(*ins)
    outs = pl.pallas_call(
        hand_over,
        out_shape=out_shape,
        in_specs=[hbm] * 6,
        out_specs=[hbm] * 5,
        scratch_shapes=[
            pltpu.VMEM((1, COLS), jnp.int32), *(pltpu.VMEM(a.shape, a.dtype) for a in out_shape), big, dma((2, 8))
        ],
        compiler_params=pltpu.CompilerParams(vmem_limit_bytes=56 * 2**20),
        name="outputs",
    )(ins[4], *outs)
    return (outs[0].reshape(state.shape), *outs[1:])


def solution(mesh):
    placed = (
        P("blk", "sec", "lev"),
        P("blk", "sec", "lev"),
        P("blk", "sec", "lev"),
        P(),
        P(("sec", "blk")),
        P(("sec", "blk", "lev"), None),
        P(("sec", "blk", "lev"), None),
        P(("sec", "blk", "lev")),
        P(None, ("sec", "blk", "lev")),
        P(),
    )
    return jax.shard_map(
        on_device,
        mesh=mesh,
        in_specs=placed,
        out_specs=(
            P("blk", "sec", "lev"),
            P(("sec", "blk", "lev"), None),
            P(("sec", "blk", "lev"), None),
            P(None, ("sec", "blk", "lev")),
            P("blk", "sec"),
        ),
        check_vma=False,
    )
```
